32 devices in a mesh: groups: 2 (over y), sector: 16 (over z, x, core).
Axes of the slice: x: 2, y: 2, z: 4, core: 2. Of those that a mesh axis runs over, the one named last changes fastest.
Arguments:
- wavefunction: bfloat16 [32768, 128], P(('groups', 'sector')), parts along dimension 0, may hold values from -90 to 90
- env_left: bfloat16 [256, 40, 128, 128], P(('groups', 'sector')), parts along dimension 0, may hold values from -3 to 3
- right_environment_terms: bfloat16 [80, 128, 128], P('groups'), parts along dimension 0, may hold values from -1 to 1
- source_tile_lookup: int32 [256, 10], P('groups'), parts along dimension 0, may hold values from 0 to 127, as said below
Outputs:
- image_three: float32 [32768, 128], P(('groups', 'sector')), parts along dimension 0
- projected: float32 [6, 3], P('groups'), parts along dimension 0
The draws below stay inside these ranges and needn't reach their ends.
There are 2 independent parts, one for each index of `groups`. The reference program is written for one: setup_inputs(seed, part) draws one part's arguments, and reference() takes and returns one part's arrays. A program takes and returns all parts, laid end to end along the dimension named above; each array names one. Nothing has to cross between parts.
Inputs may be any that keep to these rules, and one draw needn't show every extreme that they name: `source_tile_lookup`: entry 0 of output tile i is i itself. Of the other 8 x (9) entries of one device's output tiles, none names a tile of that device, at most 10 name tiles held by any one other device, and exactly 10 for some device.
All inputs are finite; a program needn't handle non-finite values.
Results may differ from the reference program's by a relative error of at most 0.0076.
Values may be sent and summed in bfloat16 or wider, within the bound.
No kernel may reach another device: no remote copies, remote signals or barrier semaphores. Data moves between devices by JAX's collectives and lax.ppermute only.
A program may use at most 128 MiB of HBM per device.

```python
import jax
import jax.numpy as jnp
from jax import lax

TILE = 128
COLS = 128
SHIFTS = 10
GROUP = 4
TERMS = 40
TILE_DEV = 8
TILES = 128
ROWS = 16384
CAP = 10
N_SECTOR = 16


def draw_wavefunction(key, part):
    key = jax.random.fold_in(key, 11)
    keys = jax.random.split(key, 3)
    rise = jnp.sqrt(1.0 + 2.0 * jnp.arange(ROWS, dtype=jnp.float32) / (ROWS - 1))
    row_scale = jnp.exp(jax.random.uniform(keys[0], (ROWS,), minval=0.0, maxval=2.3026))
    col_scale = jnp.exp(jax.random.uniform(keys[1], (COLS,), minval=0.0, maxval=2.3026))
    base = jnp.clip(jax.random.normal(keys[2], (ROWS, COLS)), -5.0, 5.0)
    entry_values = base * (rise * row_scale)[:, None] * col_scale[None, :] * 0.07
    return entry_values.astype(jnp.bfloat16)


def draw_env_left(key, part):
    key = jax.random.fold_in(key, 31)
    keys = jax.random.split(key, 2)
    noise = jnp.clip(jax.random.normal(keys[0], (TILES, TERMS, TILE, TILE)), -6.0, 6.0) / jnp.sqrt(float(TILE))
    level = jax.random.uniform(keys[1], (TILES, GROUP), minval=0.8, maxval=1.2)
    boost = jnp.concatenate([level, jnp.zeros((TILES, TERMS - GROUP), jnp.float32)], axis=1)
    identity_tile = jnp.eye(TILE, dtype=jnp.float32)
    entry_values = noise + boost[:, :, None, None] * identity_tile[None, None, :, :]
    return entry_values.astype(jnp.bfloat16)


def draw_right_environment_terms(key, part):
    key = jax.random.fold_in(key, 37)
    keys = jax.random.split(key, 2)
    noise = jnp.clip(jax.random.normal(keys[0], (TERMS, COLS, COLS)), -6.0, 6.0) / jnp.sqrt(float(TERMS * COLS))
    level = jax.random.uniform(keys[1], (GROUP,), minval=0.1, maxval=0.15)
    boost = jnp.concatenate([level, jnp.zeros((TERMS - GROUP,), jnp.float32)])
    identity_cols = jnp.eye(COLS, dtype=jnp.float32)
    entry_values = noise + boost[:, None, None] * identity_cols[None, :, :]
    return entry_values.astype(jnp.bfloat16)


def shuffle_count(key, length):
    return jax.random.permutation(key, length)


def draw_source_tile_lookup(key, part):
    key = jax.random.fold_in(key, 23)
    keys = jax.random.split(key, 3)
    others = TILE_DEV * (SHIFTS - 1)
    peer_order = jax.vmap(partial_devices)(jax.random.split(keys[0], N_SECTOR))
    readers = jnp.arange(N_SECTOR, dtype=jnp.int32)[:, None]
    peer_ids = peer_order + (peer_order >= readers).astype(jnp.int32)
    record_order = jax.vmap(partial_records)(jax.random.split(keys[1], N_SECTOR))
    source_device = jnp.take_along_axis(peer_ids, record_order // CAP, axis=1)
    local_tile = jax.random.randint(keys[2], (N_SECTOR, others), 0, TILE_DEV)
    distant = (source_device * TILE_DEV + local_tile).reshape(TILES, SHIFTS - 1).astype(jnp.int32)
    own_tile = jnp.arange(TILES, dtype=jnp.int32)[:, None]
    return jnp.concatenate([own_tile, distant], axis=1).astype(jnp.int32)


def partial_devices(key):
    return shuffle_count(key, N_SECTOR - 1).astype(jnp.int32)


def partial_records(key):
    return shuffle_count(key, TILE_DEV * (SHIFTS - 1)).astype(jnp.int32)


def setup_inputs(seed: int = 0, part: int = 0) -> dict:
    streams_of = jax.random.split(jax.random.key(seed), 5)
    part_keys = jax.random.split(jax.random.fold_in(streams_of[4], part), 5)
    wavefunction = draw_wavefunction(jax.random.fold_in(jax.random.fold_in(streams_of[4], part), 71), part)
    env_left = draw_env_left(jax.random.fold_in(jax.random.fold_in(streams_of[4], part), 71), part)
    right_environment_terms = draw_right_environment_terms(jax.random.fold_in(jax.random.fold_in(streams_of[4], part), 71), part)
    source_tile_lookup = draw_source_tile_lookup(jax.random.fold_in(jax.random.fold_in(streams_of[4], part), 71), part)
    return dict(wavefunction=wavefunction, env_left=env_left, right_environment_terms=right_environment_terms, source_tile_lookup=source_tile_lookup)


epsilon = 1e-06

def apply_operator(vector, env_left, right_environment_terms, source_tile_lookup):
    tile_stack = vector.astype(jnp.bfloat16).reshape(TILES, TILE, COLS)
    right_sector_group = right_environment_terms.astype(jnp.float32).reshape(SHIFTS, GROUP, COLS, COLS)

    def one_tile(inputs):
        left_block, sources = inputs
        picked = tile_stack[sources].astype(jnp.float32)
        left_group = left_block.astype(jnp.float32).reshape(SHIFTS, GROUP, TILE, TILE)
        left_contracted_state = jnp.einsum('ktab,kbc->ktac', left_group, picked).astype(jnp.bfloat16)
        return jnp.einsum('ktac,ktcd->ad', left_contracted_state.astype(jnp.float32), right_sector_group)
    product = lax.map(one_tile, (env_left, source_tile_lookup))
    return product.reshape(ROWS, COLS)

def mean_product(first, second):
    return jnp.sum(first * second) / (ROWS * COLS)

def reference(wavefunction, env_left, right_environment_terms, source_tile_lookup):
    start = wavefunction.astype(jnp.float32)
    basis_one = start * lax.rsqrt(mean_product(start, start) + epsilon)
    first_krylov_image = apply_operator(basis_one, env_left, right_environment_terms, source_tile_lookup)
    coef_aa = mean_product(basis_one, first_krylov_image)
    remainder = first_krylov_image - coef_aa * basis_one
    coef_ba = jnp.sqrt(mean_product(remainder, remainder) + epsilon)
    basis_two = remainder / coef_ba
    image_two = apply_operator(basis_two, env_left, right_environment_terms, source_tile_lookup)
    coef_ab = mean_product(basis_one, image_two)
    coef_bb = mean_product(basis_two, image_two)
    remainder = image_two - coef_ab * basis_one - coef_bb * basis_two
    coef_cb = jnp.sqrt(mean_product(remainder, remainder) + epsilon)
    basis_three = remainder / coef_cb
    image_three = apply_operator(basis_three, env_left, right_environment_terms, source_tile_lookup)
    coef_ac = mean_product(basis_one, image_three)
    coef_bc = mean_product(basis_two, image_three)
    coef_cc = mean_product(basis_three, image_three)
    zero_entry = jnp.zeros((), jnp.float32)
    projected = jnp.stack([jnp.stack([coef_aa, coef_ab, coef_ac]), jnp.stack([coef_ba, coef_bb, coef_bc]), jnp.stack([zero_entry, coef_cb, coef_cc])])
    return (image_three, projected)
```

```python
import functools

import jax
import jax.numpy as jnp
from jax import lax
from jax.experimental import pallas as pl
from jax.experimental.pallas import tpu as pltpu
from jax.sharding import PartitionSpec as P

epsilon = 1e-06
f32 = jnp.float32
bf16 = jnp.bfloat16
STAT_ROWS = 16


def row(value):
    return jnp.broadcast_to(value, (1, 128))


def lane_sums(product):
    return jnp.sum(product, axis=0, keepdims=True)


def split_rows(sums):
    rows = []
    for value in sums:
        high = value.astype(bf16)
        rest = value - high.astype(f32)
        middle = rest.astype(bf16)
        low = (rest - middle.astype(f32)).astype(bf16)
        rows += [high, middle, low]
    rows += [jnp.zeros((1, 128), bf16)] * (STAT_ROWS - len(rows))
    return jnp.concatenate([r.astype(f32) for r in rows], axis=0).astype(bf16)


def start_kernel(w_ref, piece_ref):
    rows = w_ref.shape[0]
    w = w_ref[...]
    piece_ref[0:rows, :] = w
    wide = w.astype(f32)
    piece_ref[rows:, :] = split_rows([lane_sums(wide * wide)])


def load_kernel(env_ref, right_ref, env_out, right_out, sems):
    parts = 8
    step = env_ref.shape[0] // parts
    copies = [
        pltpu.make_async_copy(
            env_ref.at[pl.ds(j * step, step)], env_out.at[pl.ds(j * step, step)], sems.at[j]
        )
        for j in range(parts)
    ]
    copies.append(pltpu.make_async_copy(right_ref, right_out, sems.at[parts]))
    for copy in copies:
        copy.start()
    for copy in copies:
        copy.wait()


def apply_kernel(stage, sizes, tile_ref, stat_ref, buf_ref, env_ref, right_ref, w_ref, *rest):
    tile_dev, shifts, group, tile_rows, total = sizes
    prior = rest[: stage - 1]
    rest = rest[stage - 1 :]
    if stage > 1:
        coef_in, rest = rest[0], rest[1:]
    image_ref, coef_ref, send_ref, left_ref = rest
    width = group * tile_rows

    def one_tile(i, carry):
        for k in range(shifts):
            offset = pl.multiple_of(tile_ref[i * shifts + k], 16)
            picked = buf_ref[pl.ds(offset, tile_rows), :]
            start = pl.multiple_of((i * shifts + k) * width, width)
            product = jnp.dot(
                env_ref[pl.ds(start, width), :], picked, preferred_element_type=f32
            ).astype(bf16)
            for t in range(group):
                left_ref[
                    pl.ds(pl.multiple_of(i * tile_rows, tile_rows), tile_rows),
                    (k * group + t) * 128 : (k * group + t + 1) * 128,
                ] = product[t * tile_rows : (t + 1) * tile_rows]
        return carry

    lax.fori_loop(0, tile_dev, one_tile, 0)
    applied = jnp.dot(left_ref[...], right_ref[...], preferred_element_type=f32)

    gathered = jnp.zeros((STAT_ROWS, 128), f32)
    for d in range(stat_ref.shape[0]):
        offset = pl.multiple_of(stat_ref[d], 16)
        gathered = gathered + buf_ref[pl.ds(offset, STAT_ROWS), :].astype(f32)

    def mean_of(j):
        lanes = gathered[3 * j : 3 * j + 1] + gathered[3 * j + 1 : 3 * j + 2]
        lanes = lanes + gathered[3 * j + 2 : 3 * j + 3]
        return row(jnp.sum(lanes, axis=1, keepdims=True) * (1.0 / total))

    w = w_ref[...].astype(f32)
    if stage == 1:
        square = mean_of(0)
        scale = lax.rsqrt(square + epsilon)
        coefs = [scale, scale * scale * square]
        image = scale * applied
        sums = [lane_sums((w * scale) * image), lane_sums(image * image)]
    elif stage == 2:
        scale, g11 = coef_in[0:1, :], coef_in[1:2, :]
        aa, norm = mean_of(0), mean_of(1)
        rest_square = jnp.maximum(norm - 2.0 * aa * aa + aa * aa * g11, 0.0)
        ba = jnp.sqrt(rest_square + epsilon)
        g12 = (aa - aa * g11) / ba
        g22 = rest_square / (ba * ba)
        coefs = [scale, g11, aa, ba, g12, g22]
        first = prior[0][...]
        basis_one = w * scale
        basis_two = (first - aa * basis_one) / ba
        image = (applied - aa * first) / ba
        sums = [
            lane_sums(basis_one * image),
            lane_sums(basis_two * image),
            lane_sums(image * image),
        ]
    else:
        scale, g11, aa, ba, g12, g22 = [coef_in[j : j + 1, :] for j in range(6)]
        ab, bb, norm = mean_of(0), mean_of(1), mean_of(2)
        rest_square = norm - 2.0 * (ab * ab + bb * bb) + ab * ab * g11 + bb * bb * g22
        rest_square = jnp.maximum(rest_square + 2.0 * ab * bb * g12, 0.0)
        cb = jnp.sqrt(rest_square + epsilon)
        coefs = [aa, ab, ba, bb, cb]
        first, second = prior[0][...], prior[1][...]
        basis_one = w * scale
        basis_two = (first - aa * basis_one) / ba
        basis_three = (second - ab * basis_one - bb * basis_two) / cb
        image = (applied - ab * first - bb * second) / cb
        sums = [lane_sums(b * image) for b in (basis_one, basis_two, basis_three)]

    image_ref[...] = image
    coef_ref[...] = jnp.concatenate(coefs + [jnp.zeros((1, 128), f32)] * (8 - len(coefs)), axis=0)
    if stage < 3:
        rows = image.shape[0]
        send_ref[0:rows, :] = image.astype(bf16)
        send_ref[rows:, :] = split_rows(sums)
    else:
        send_ref[...] = jnp.concatenate(sums + [jnp.zeros((1, 128), f32)] * 5, axis=0)


def finish_kernel(total, stat_ref, coef_ref, out_ref):
    last = [row(jnp.sum(stat_ref[j : j + 1, :], axis=1, keepdims=True) * (1.0 / total)) for j in range(3)]
    aa, ab, ba, bb, cb = [coef_ref[j : j + 1, :] for j in range(5)]
    lane = lax.broadcasted_iota(jnp.int32, (1, 128), 1)

    def line(a, b, c):
        return jnp.where(lane == 0, a, jnp.where(lane == 1, b, c))

    zero = jnp.zeros((1, 128), f32)
    table = jnp.concatenate(
        [line(aa, ab, last[0]), line(ba, bb, last[1]), line(zero, cb, last[2])], axis=0
    )
    out_ref[...] = table[:, 0:3]


def ring_pairs(peers):
    chips = peers // 2
    order = list(range(0, chips, 2)) + list(range(chips - 1, 0, -2))
    forward = [
        (order[j] * 2 + c, order[(j + 1) % chips] * 2 + c) for j in range(chips) for c in range(2)
    ]
    return forward, [(b, a) for a, b in forward]


def ring_place(chip, chips):
    return jnp.where(chip % 2 == 0, chip // 2, chips - 1 - chip // 2)


def per_device(wavefunction, env_left, right_environment_terms, source_tile_lookup):
    peers = lax.axis_size("sector")
    own = lax.axis_index("sector")
    tile_dev, terms, tile_rows = env_left.shape[0], env_left.shape[1], env_left.shape[2]
    rows, columns = wavefunction.shape
    shifts = source_tile_lookup.shape[1]
    records = tile_dev * shifts
    total = peers * rows * columns
    sizes = (tile_dev, shifts, terms // shifts, tile_rows, total)
    piece_rows = rows + STAT_ROWS
    lookup = source_tile_lookup
    own_records = lax.dynamic_slice_in_dim(lookup, own * tile_dev, tile_dev, 0).reshape(records)
    source = own_records // tile_dev
    local = own_records % tile_dev
    devices = jnp.arange(peers, dtype=jnp.int32)
    use_ring = peers * tile_dev <= 2 * records

    if use_ring:
        chips = peers // 2
        forward, backward = ring_pairs(peers)
        sibling = [(i, i ^ 1) for i in range(peers)]
        here = ring_place(own // 2, chips)

        def slot_of(device):
            steps = (ring_place(device // 2, chips) - here) % chips
            return steps * 2 + (device % 2 + own % 2) % 2

        tile_offset = slot_of(source) * piece_rows + local * tile_rows
        stat_offset = slot_of(devices) * piece_rows + rows

        def exchange(piece):
            pieces = {0: piece}
            ahead = behind = piece
            for step in range(1, chips // 2 + 1):
                ahead = lax.ppermute(ahead, "sector", forward)
                pieces[chips - step] = ahead
                if 2 * step < chips:
                    behind = lax.ppermute(behind, "sector", backward)
                    pieces[step] = behind
            parts = []
            for j in range(chips):
                parts += [pieces[j], lax.ppermute(pieces[j], "sector", sibling)]
            return jnp.concatenate(parts, axis=0)

    else:
        capacity = max(1, 2 * records // peers)
        is_self = source == own
        hot = ((source[:, None] == devices[None, :]) & ~is_self[:, None]).astype(jnp.int32)
        rank = jnp.sum(hot * jnp.cumsum(hot, axis=0), axis=1) - 1
        every = lookup.reshape(peers, records)
        wanted = ((every // tile_dev == own) & (devices != own)[:, None]).astype(jnp.int32)
        order = jnp.cumsum(wanted, axis=1) - 1
        slots = jnp.arange(capacity, dtype=jnp.int32)
        chosen = wanted[:, :, None] * (order[:, :, None] == slots).astype(jnp.int32)
        send_index = jnp.sum(chosen * (every % tile_dev)[:, :, None], axis=1).reshape(-1)
        place = jnp.where(is_self, local, tile_dev + source * capacity + rank)
        tile_offset = place * tile_rows
        stat_base = (tile_dev + peers * capacity) * tile_rows
        stat_offset = stat_base + devices * STAT_ROWS

        def exchange(piece):
            tiles = piece[:rows].reshape(tile_dev, tile_rows, columns)
            incoming = lax.all_to_all(tiles[send_index], "sector", 0, 0, tiled=True)
            stats = lax.all_gather(piece[rows:], "sector", axis=0, tiled=True)
            return jnp.concatenate([piece[:rows], incoming.reshape(-1, columns), stats], axis=0)

    vmem = pl.BlockSpec(memory_space=pltpu.VMEM)
    smem = pl.BlockSpec(memory_space=pltpu.SMEM)
    hbm = pl.BlockSpec(memory_space=pl.ANY)

    piece = pl.pallas_call(
        start_kernel,
        out_shape=jax.ShapeDtypeStruct((piece_rows, columns), bf16),
        in_specs=[vmem],
        out_specs=vmem,
        compiler_params=pltpu.CompilerParams(vmem_limit_bytes=4 * 2**20),
    )(wavefunction)
    env_flat = env_left.reshape(tile_dev * terms * tile_rows, tile_rows)
    right_flat = right_environment_terms.reshape(terms * columns, columns)
    env_near, right_near = pl.pallas_call(
        load_kernel,
        out_shape=(pltpu.VMEM(env_flat.shape, bf16), pltpu.VMEM(right_flat.shape, bf16)),
        in_specs=[hbm, hbm],
        out_specs=(vmem, vmem),
        scratch_shapes=[pltpu.SemaphoreType.DMA((9,))],
        compiler_params=pltpu.CompilerParams(vmem_limit_bytes=2 * 2**20),
    )(env_flat, right_flat)

    def apply_operator(stage, buffer, prior, coefs):
        image = jax.ShapeDtypeStruct((rows, columns), f32)
        small = jax.ShapeDtypeStruct((8, 128), f32)
        send = small if stage == 3 else jax.ShapeDtypeStruct((piece_rows, columns), bf16)
        operands = [buffer, env_near, right_near, wavefunction, *prior, *coefs]
        return pl.pallas_call(
            functools.partial(apply_kernel, stage, sizes),
            out_shape=(image, small, send),
            in_specs=[smem, smem] + [vmem] * len(operands),
            out_specs=(vmem, vmem, vmem),
            scratch_shapes=[pltpu.VMEM((rows, terms * columns), bf16)],
            compiler_params=pltpu.CompilerParams(vmem_limit_bytes=20 * 2**20),
            cost_estimate=pl.CostEstimate(
                flops=4 * rows * terms * tile_rows * columns, bytes_accessed=2**24, transcendentals=0
            ),
        )(tile_offset, stat_offset, *operands)

    image_one, coefs_one, piece = apply_operator(1, exchange(piece), [], [])
    image_two, coefs_two, piece = apply_operator(2, exchange(piece), [image_one], [coefs_one])
    image_three, coefs_three, stats = apply_operator(
        3, exchange(piece), [image_one, image_two], [coefs_two]
    )
    distance = 1
    while distance < peers:
        pairs = [(i, i ^ distance) for i in range(peers)]
        stats = stats + lax.ppermute(stats, "sector", pairs)
        distance *= 2
    projected = pl.pallas_call(
        functools.partial(finish_kernel, total),
        out_shape=jax.ShapeDtypeStruct((3, 3), f32),
        in_specs=[vmem, vmem],
        out_specs=vmem,
        compiler_params=pltpu.CompilerParams(vmem_limit_bytes=2 * 2**20),
    )(stats, coefs_three)
    return (image_three, projected)


def solution(mesh):
    return jax.shard_map(
        per_device,
        mesh=mesh,
        in_specs=(
            P(("groups", "sector"), None),
            P(("groups", "sector"), None, None, None),
            P("groups", None, None),
            P("groups", None),
        ),
        out_specs=(P(("groups", "sector"), None), P("groups", None)),
        check_vma=False,
    )
```

```python
import functools

import jax
import jax.numpy as jnp
from jax import lax
from jax.experimental import pallas as pl
from jax.experimental.pallas import tpu as pltpu
from jax.sharding import PartitionSpec as P

epsilon = 1e-06
f32 = jnp.float32
bf16 = jnp.bfloat16
STAT_ROWS = 16


def row(value):
    return jnp.broadcast_to(value, (1, 128))


def lane_sums(product):
    return jnp.sum(product, axis=0, keepdims=True)


def split_rows(sums):
    rows = []
    for value in sums:
        high = value.astype(bf16)
        rest = value - high.astype(f32)
        middle = rest.astype(bf16)
        low = (rest - middle.astype(f32)).astype(bf16)
        rows += [high, middle, low]
    rows += [jnp.zeros((1, 128), bf16)] * (STAT_ROWS - len(rows))
    return jnp.concatenate([r.astype(f32) for r in rows], axis=0).astype(bf16)


def start_kernel(w_ref, piece_ref):
    rows = w_ref.shape[0]
    w = w_ref[...]
    piece_ref[0:rows, :] = w
    wide = w.astype(f32)
    piece_ref[rows:, :] = split_rows([lane_sums(wide * wide)])


def load_kernel(env_ref, right_ref, env_out, right_out, sems):
    parts = 8
    step = env_ref.shape[0] // parts
    copies = [
        pltpu.make_async_copy(
            env_ref.at[pl.ds(j * step, step)], env_out.at[pl.ds(j * step, step)], sems.at[j]
        )
        for j in range(parts)
    ]
    copies.append(pltpu.make_async_copy(right_ref, right_out, sems.at[parts]))
    for copy in copies:
        copy.start()
    for copy in copies:
        copy.wait()


def apply_kernel(stage, sizes, tile_ref, stat_ref, buf_ref, env_ref, right_ref, w_ref, *rest):
    tile_dev, shifts, group, tile_rows, total = sizes
    prior = rest[: stage - 1]
    rest = rest[stage - 1 :]
    if stage > 1:
        coef_in, rest = rest[0], rest[1:]
    image_ref, coef_ref, send_ref, left_ref = rest
    width = group * tile_rows

    def one_tile(i, carry):
        for k in range(shifts):
            offset = pl.multiple_of(tile_ref[i * shifts + k], 16)
            picked = buf_ref[pl.ds(offset, tile_rows), :]
            start = pl.multiple_of((i * shifts + k) * width, width)
            product = jnp.dot(
                env_ref[pl.ds(start, width), :], picked, preferred_element_type=f32
            ).astype(bf16)
            for t in range(group):
                left_ref[
                    pl.ds(pl.multiple_of(i * tile_rows, tile_rows), tile_rows),
                    (k * group + t) * 128 : (k * group + t + 1) * 128,
                ] = product[t * tile_rows : (t + 1) * tile_rows]
        return carry

    lax.fori_loop(0, tile_dev, one_tile, 0)
    applied = jnp.dot(left_ref[...], right_ref[...], preferred_element_type=f32)

    gathered = jnp.zeros((STAT_ROWS, 128), f32)
    for d in range(stat_ref.shape[0]):
        offset = pl.multiple_of(stat_ref[d], 16)
        gathered = gathered + buf_ref[pl.ds(offset, STAT_ROWS), :].astype(f32)

    def mean_of(j):
        lanes = gathered[3 * j : 3 * j + 1] + gathered[3 * j + 1 : 3 * j + 2]
        lanes = lanes + gathered[3 * j + 2 : 3 * j + 3]
        return row(jnp.sum(lanes, axis=1, keepdims=True) * (1.0 / total))

    w = w_ref[...].astype(f32)
    if stage == 1:
        square = mean_of(0)
        scale = lax.rsqrt(square + epsilon)
        coefs = [scale, scale * scale * square]
        image = scale * applied
        sums = [lane_sums((w * scale) * image), lane_sums(image * image)]
    elif stage == 2:
        scale, g11 = coef_in[0:1, :], coef_in[1:2, :]
        aa, norm = mean_of(0), mean_of(1)
        rest_square = jnp.maximum(norm - 2.0 * aa * aa + aa * aa * g11, 0.0)
        ba = jnp.sqrt(rest_square + epsilon)
        g12 = (aa - aa * g11) / ba
        g22 = rest_square / (ba * ba)
        coefs = [scale, g11, aa, ba, g12, g22]
        first = prior[0][...]
        basis_one = w * scale
        basis_two = (first - aa * basis_one) / ba
        image = (applied - aa * first) / ba
        sums = [
            lane_sums(basis_one * image),
            lane_sums(basis_two * image),
            lane_sums(image * image),
        ]
    else:
        scale, g11, aa, ba, g12, g22 = [coef_in[j : j + 1, :] for j in range(6)]
        ab, bb, norm = mean_of(0), mean_of(1), mean_of(2)
        rest_square = norm - 2.0 * (ab * ab + bb * bb) + ab * ab * g11 + bb * bb * g22
        rest_square = jnp.maximum(rest_square + 2.0 * ab * bb * g12, 0.0)
        cb = jnp.sqrt(rest_square + epsilon)
        coefs = [aa, ab, ba, bb, cb]
        first, second = prior[0][...], prior[1][...]
        basis_one = w * scale
        basis_two = (first - aa * basis_one) / ba
        basis_three = (second - ab * basis_one - bb * basis_two) / cb
        image = (applied - ab * first - bb * second) / cb
        sums = [lane_sums(b * image) for b in (basis_one, basis_two, basis_three)]

    image_ref[...] = image
    coef_ref[...] = jnp.concatenate(coefs + [jnp.zeros((1, 128), f32)] * (8 - len(coefs)), axis=0)
    if stage < 3:
        rows = image.shape[0]
        send_ref[0:rows, :] = image.astype(bf16)
        send_ref[rows:, :] = split_rows(sums)
    else:
        send_ref[...] = jnp.concatenate(sums + [jnp.zeros((1, 128), f32)] * 5, axis=0)


def finish_kernel(total, stat_ref, coef_ref, out_ref):
    last = [row(jnp.sum(stat_ref[j : j + 1, :], axis=1, keepdims=True) * (1.0 / total)) for j in range(3)]
    aa, ab, ba, bb, cb = [coef_ref[j : j + 1, :] for j in range(5)]
    lane = lax.broadcasted_iota(jnp.int32, (1, 128), 1)

    def line(a, b, c):
        return jnp.where(lane == 0, a, jnp.where(lane == 1, b, c))

    zero = jnp.zeros((1, 128), f32)
    table = jnp.concatenate(
        [line(aa, ab, last[0]), line(ba, bb, last[1]), line(zero, cb, last[2])], axis=0
    )
    out_ref[...] = table[:, 0:3]


def ring_pairs(peers):
    chips = peers // 2
    order = list(range(0, chips, 2)) + list(range(chips - 1, 0, -2))
    pairs = []
    for j in range(chips):
        here, after = order[j] * 2, order[(j + 1) % chips] * 2
        pairs += [(here, after), (after + 1, here + 1)]
    return pairs


def ring_place(chip, chips):
    return jnp.where(chip % 2 == 0, chip // 2, chips - 1 - chip // 2)


def per_device(wavefunction, env_left, right_environment_terms, source_tile_lookup):
    peers = lax.axis_size("sector")
    own = lax.axis_index("sector")
    tile_dev, terms, tile_rows = env_left.shape[0], env_left.shape[1], env_left.shape[2]
    rows, columns = wavefunction.shape
    shifts = source_tile_lookup.shape[1]
    records = tile_dev * shifts
    total = peers * rows * columns
    sizes = (tile_dev, shifts, terms // shifts, tile_rows, total)
    piece_rows = rows + STAT_ROWS
    lookup = source_tile_lookup
    own_records = lax.dynamic_slice_in_dim(lookup, own * tile_dev, tile_dev, 0).reshape(records)
    source = own_records // tile_dev
    local = own_records % tile_dev
    devices = jnp.arange(peers, dtype=jnp.int32)
    use_ring = peers * tile_dev <= 2 * records

    if use_ring:
        chips = peers // 2
        onward = ring_pairs(peers)
        sibling = [(i, i ^ 1) for i in range(peers)]
        core = own % 2
        here = ring_place(own // 2, chips)

        def slot_of(device):
            ahead = (here - ring_place(device // 2, chips)) % chips
            steps = jnp.where(core == 0, ahead, (chips - ahead) % chips)
            other = (device + core) % 2
            half = chips // 2
            last = 2 + 4 * (half - 1)
            direct = 2 + 4 * (steps - 1) + 2 * other
            passed = 2 + 4 * (chips - steps - 1) + 3 - 2 * other
            slot = jnp.where(steps < half, direct, passed)
            slot = jnp.where(steps == half, last + other, slot)
            return jnp.where(steps == 0, other, slot)

        tile_offset = slot_of(source) * piece_rows + local * tile_rows
        stat_offset = slot_of(devices) * piece_rows + rows

        def exchange(piece):
            first, second = lax.optimization_barrier(
                (piece, lax.ppermute(piece, "sector", sibling))
            )
            parts = [first, second]
            for step in range(1, chips // 2 + 1):
                first = lax.ppermute(first, "sector", onward)
                parts += [first, lax.ppermute(first, "sector", sibling)]
                if 2 * step < chips:
                    second = lax.ppermute(second, "sector", onward)
                    parts += [second, lax.ppermute(second, "sector", sibling)]
            return jnp.concatenate(parts, axis=0)

    else:
        capacity = max(1, 2 * records // peers)
        is_self = source == own
        hot = ((source[:, None] == devices[None, :]) & ~is_self[:, None]).astype(jnp.int32)
        rank = jnp.sum(hot * jnp.cumsum(hot, axis=0), axis=1) - 1
        every = lookup.reshape(peers, records)
        wanted = ((every // tile_dev == own) & (devices != own)[:, None]).astype(jnp.int32)
        order = jnp.cumsum(wanted, axis=1) - 1
        slots = jnp.arange(capacity, dtype=jnp.int32)
        chosen = wanted[:, :, None] * (order[:, :, None] == slots).astype(jnp.int32)
        send_index = jnp.sum(chosen * (every % tile_dev)[:, :, None], axis=1).reshape(-1)
        place = jnp.where(is_self, local, tile_dev + source * capacity + rank)
        tile_offset = place * tile_rows
        stat_base = (tile_dev + peers * capacity) * tile_rows
        stat_offset = stat_base + devices * STAT_ROWS

        def exchange(piece):
            tiles = piece[:rows].reshape(tile_dev, tile_rows, columns)
            incoming = lax.all_to_all(tiles[send_index], "sector", 0, 0, tiled=True)
            stats = lax.all_gather(piece[rows:], "sector", axis=0, tiled=True)
            return jnp.concatenate([piece[:rows], incoming.reshape(-1, columns), stats], axis=0)

    vmem = pl.BlockSpec(memory_space=pltpu.VMEM)
    smem = pl.BlockSpec(memory_space=pltpu.SMEM)
    hbm = pl.BlockSpec(memory_space=pltpu.HBM)

    piece = pl.pallas_call(
        start_kernel,
        out_shape=jax.ShapeDtypeStruct((piece_rows, columns), bf16),
        in_specs=[vmem],
        out_specs=vmem,
        compiler_params=pltpu.CompilerParams(vmem_limit_bytes=4 * 2**20),
    )(wavefunction)
    env_flat = env_left.reshape(tile_dev * terms * tile_rows, tile_rows)
    right_flat = right_environment_terms.reshape(terms * columns, columns)
    env_near, right_near = pl.pallas_call(
        load_kernel,
        out_shape=(pltpu.VMEM(env_flat.shape, bf16), pltpu.VMEM(right_flat.shape, bf16)),
        in_specs=[hbm, hbm],
        out_specs=(vmem, vmem),
        scratch_shapes=[pltpu.SemaphoreType.DMA((9,))],
        compiler_params=pltpu.CompilerParams(vmem_limit_bytes=2 * 2**20),
    )(env_flat, right_flat)

    def apply_operator(stage, buffer, prior, coefs):
        image = jax.ShapeDtypeStruct((rows, columns), f32)
        small = jax.ShapeDtypeStruct((8, 128), f32)
        send = small if stage == 3 else jax.ShapeDtypeStruct((piece_rows, columns), bf16)
        operands = [buffer, env_near, right_near, wavefunction, *prior, *coefs]
        return pl.pallas_call(
            functools.partial(apply_kernel, stage, sizes),
            out_shape=(image, small, send),
            in_specs=[smem, smem] + [vmem] * len(operands),
            out_specs=(vmem, vmem, vmem),
            scratch_shapes=[pltpu.VMEM((rows, terms * columns), bf16)],
            compiler_params=pltpu.CompilerParams(vmem_limit_bytes=20 * 2**20),
            cost_estimate=pl.CostEstimate(
                flops=4 * rows * terms * tile_rows * columns, bytes_accessed=2**24, transcendentals=0
            ),
        )(tile_offset, stat_offset, *operands)

    image_one, coefs_one, piece = apply_operator(1, exchange(piece), [], [])
    image_two, coefs_two, piece = apply_operator(2, exchange(piece), [image_one], [coefs_one])
    image_three, coefs_three, stats = apply_operator(
        3, exchange(piece), [image_one, image_two], [coefs_two]
    )
    distance = 1
    while distance < peers:
        pairs = [(i, i ^ distance) for i in range(peers)]
        stats = stats + lax.ppermute(stats, "sector", pairs)
        distance *= 2
    projected = pl.pallas_call(
        functools.partial(finish_kernel, total),
        out_shape=jax.ShapeDtypeStruct((3, 3), f32),
        in_specs=[vmem, vmem],
        out_specs=vmem,
        compiler_params=pltpu.CompilerParams(vmem_limit_bytes=2 * 2**20),
    )(stats, coefs_three)
    return (image_three, projected)


def solution(mesh):
    return jax.shard_map(
        per_device,
        mesh=mesh,
        in_specs=(
            P(("groups", "sector"), None),
            P(("groups", "sector"), None, None, None),
            P("groups", None, None),
            P("groups", None),
        ),
        out_specs=(P(("groups", "sector"), None), P("groups", None)),
        check_vma=False,
    )
```

```python
import functools

import jax
import jax.numpy as jnp
from jax import lax
from jax.experimental import pallas as pl
from jax.experimental.pallas import tpu as pltpu
from jax.sharding import PartitionSpec as P

epsilon = 1e-06
f32 = jnp.float32
bf16 = jnp.bfloat16
STAT_ROWS = 16
LOADS = 4


def row(value):
    return jnp.broadcast_to(value, (1, 128))


def lane_sums(product):
    return jnp.sum(product, axis=0, keepdims=True)


def split_rows(sums):
    rows = []
    for value in sums:
        high = value.astype(bf16)
        rest = value - high.astype(f32)
        middle = rest.astype(bf16)
        low = (rest - middle.astype(f32)).astype(bf16)
        rows += [high, middle, low]
    rows += [jnp.zeros((1, 128), bf16)] * (STAT_ROWS - len(rows))
    return jnp.concatenate([r.astype(f32) for r in rows], axis=0).astype(bf16)


def start_kernel(w_ref, piece_ref):
    rows = w_ref.shape[0]
    w = w_ref[...]
    piece_ref[0:rows, :] = w
    wide = w.astype(f32)
    piece_ref[rows:, :] = split_rows([lane_sums(wide * wide)])


def prepare_kernel(sizes, phases, phase_ref, offset_ref, env_ref, *rest):
    count_ref, list_ref, env_out, sems = rest
    tile_dev, shifts, group, tile_rows, total = sizes
    records = tile_dev * shifts
    step = env_ref.shape[0] // LOADS
    copies = []
    for j in range(LOADS):
        rows = pl.ds(j * step, step)
        copies.append(pltpu.make_async_copy(env_ref.at[rows], env_out.at[rows], sems.at[j]))
    for copy in copies:
        copy.start()
    for p in range(phases):
        count_ref[p] = 0

    def one_tile(tile, carry):
        for shift in range(shifts):
            r = tile * shifts + shift
            p = phase_ref[r]
            n = count_ref[p]
            list_ref[0, p * records + n] = offset_ref[r]
            list_ref[1, p * records + n] = r * group * tile_rows
            list_ref[2, p * records + n] = (shift * tile_dev + tile) * tile_rows
            count_ref[p] = n + 1
        return carry

    lax.fori_loop(0, tile_dev, one_tile, 0)
    for copy in copies:
        copy.wait()


def contract_left(phase, unroll, sizes, count_ref, list_ref, buf_ref, env_ref, left_ref):
    tile_dev, shifts, group, tile_rows, total = sizes
    base = phase * tile_dev * shifts
    width = group * tile_rows
    count = count_ref[phase]

    def one(n):
        offset = pl.multiple_of(list_ref[0, n], 16)
        start = pl.multiple_of(list_ref[1, n], 128)
        target = pl.multiple_of(list_ref[2, n], 128)
        picked = buf_ref[pl.ds(offset, tile_rows), :]
        for t in range(group):
            left_ref[pl.ds(target, tile_rows), t * 128 : (t + 1) * 128] = jnp.dot(
                env_ref[pl.ds(start + t * tile_rows, tile_rows), :],
                picked,
                preferred_element_type=f32,
            ).astype(bf16)

    def many(j, carry):
        for q in range(unroll):
            one(base + j * unroll + q)
        return carry

    def few(j, carry):
        for q in range(4):
            one(base + jnp.minimum(whole * unroll + j * 4 + q, count - 1))
        return carry

    whole = count // unroll
    lax.fori_loop(0, whole, many, 0)
    lax.fori_loop(0, (count - whole * unroll + 3) // 4, few, 0)


def left_kernel(phase, unroll, sizes, count_ref, list_ref, buf_ref, env_ref, *rest):
    contract_left(phase, unroll, sizes, count_ref, list_ref, buf_ref, env_ref, rest[-1])


def apply_kernel(stage, sizes, slots, stat_ref, right_ref, w_ref, *rest):
    tile_dev, shifts, group, tile_rows, total = sizes
    rows = tile_dev * tile_rows
    phases = max(p for p, _ in slots) + 1
    bufs, rest = rest[:phases], rest[phases:]
    prior, rest = rest[: stage - 1], rest[stage - 1 :]
    if stage > 1:
        coef_in, rest = rest[0], rest[1:]
    left_ref, image_ref, coef_ref, send_ref, all_stats = rest

    width = group * tile_rows
    applied = jnp.zeros((rows, 128), f32)
    for k in range(shifts):
        applied = applied + jnp.dot(
            left_ref[k * rows : (k + 1) * rows, :],
            right_ref[k * width : (k + 1) * width, :],
            preferred_element_type=f32,
        )

    for n, (p, offset) in enumerate(slots):
        all_stats[n * STAT_ROWS : (n + 1) * STAT_ROWS, :] = bufs[p][offset : offset + STAT_ROWS, :]
    gathered = jnp.zeros((STAT_ROWS, 128), f32)
    for d in range(stat_ref.shape[0]):
        offset = pl.multiple_of(stat_ref[d], 16)
        gathered = gathered + all_stats[pl.ds(offset, STAT_ROWS), :].astype(f32)

    def mean_of(j):
        lanes = gathered[3 * j : 3 * j + 1] + gathered[3 * j + 1 : 3 * j + 2]
        lanes = lanes + gathered[3 * j + 2 : 3 * j + 3]
        return row(jnp.sum(lanes, axis=1, keepdims=True) * (1.0 / total))

    w = w_ref[...].astype(f32)
    if stage == 1:
        square = mean_of(0)
        scale = lax.rsqrt(square + epsilon)
        coefs = [scale, scale * scale * square]
        image = scale * applied
        sums = [lane_sums((w * scale) * image), lane_sums(image * image)]
    elif stage == 2:
        scale, g11 = coef_in[0:1, :], coef_in[1:2, :]
        aa, norm = mean_of(0), mean_of(1)
        rest_square = jnp.maximum(norm - 2.0 * aa * aa + aa * aa * g11, 0.0)
        ba = jnp.sqrt(rest_square + epsilon)
        g12 = (aa - aa * g11) / ba
        g22 = rest_square / (ba * ba)
        coefs = [scale, g11, aa, ba, g12, g22]
        first = prior[0][...]
        basis_one = w * scale
        basis_two = (first - aa * basis_one) / ba
        image = (applied - aa * first) / ba
        sums = [
            lane_sums(basis_one * image),
            lane_sums(basis_two * image),
            lane_sums(image * image),
        ]
    else:
        scale, g11, aa, ba, g12, g22 = [coef_in[j : j + 1, :] for j in range(6)]
        ab, bb, norm = mean_of(0), mean_of(1), mean_of(2)
        rest_square = norm - 2.0 * (ab * ab + bb * bb) + ab * ab * g11 + bb * bb * g22
        rest_square = jnp.maximum(rest_square + 2.0 * ab * bb * g12, 0.0)
        cb = jnp.sqrt(rest_square + epsilon)
        coefs = [aa, ab, ba, bb, cb]
        first, second = prior[0][...], prior[1][...]
        basis_one = w * scale
        basis_two = (first - aa * basis_one) / ba
        basis_three = (second - ab * basis_one - bb * basis_two) / cb
        image = (applied - ab * first - bb * second) / cb
        sums = [lane_sums(b * image) for b in (basis_one, basis_two, basis_three)]

    image_ref[...] = image
    coef_ref[...] = jnp.concatenate(coefs + [jnp.zeros((1, 128), f32)] * (8 - len(coefs)), axis=0)
    if stage < 3:
        rows = image.shape[0]
        send_ref[0:rows, :] = image.astype(bf16)
        send_ref[rows:, :] = split_rows(sums)
    else:
        send_ref[...] = jnp.concatenate(sums + [jnp.zeros((1, 128), f32)] * 5, axis=0)


def finish_kernel(total, stat_ref, coef_ref, out_ref):
    last = [row(jnp.sum(stat_ref[j : j + 1, :], axis=1, keepdims=True) * (1.0 / total)) for j in range(3)]
    aa, ab, ba, bb, cb = [coef_ref[j : j + 1, :] for j in range(5)]
    lane = lax.broadcasted_iota(jnp.int32, (1, 128), 1)

    def line(a, b, c):
        return jnp.where(lane == 0, a, jnp.where(lane == 1, b, c))

    zero = jnp.zeros((1, 128), f32)
    table = jnp.concatenate(
        [line(aa, ab, last[0]), line(ba, bb, last[1]), line(zero, cb, last[2])], axis=0
    )
    out_ref[...] = table[:, 0:3]


def ring_pairs(peers):
    chips = peers // 2
    order = list(range(0, chips, 2)) + list(range(chips - 1, 0, -2))
    pairs = []
    for j in range(chips):
        here, after = order[j] * 2, order[(j + 1) % chips] * 2
        pairs += [(here, after), (after + 1, here + 1)]
    return pairs


def ring_place(chip, chips):
    return jnp.where(chip % 2 == 0, chip // 2, chips - 1 - chip // 2)


def per_device(wavefunction, env_left, right_environment_terms, source_tile_lookup):
    peers = lax.axis_size("sector")
    own = lax.axis_index("sector")
    tile_dev, terms, tile_rows = env_left.shape[0], env_left.shape[1], env_left.shape[2]
    rows, columns = wavefunction.shape
    shifts = source_tile_lookup.shape[1]
    records = tile_dev * shifts
    total = peers * rows * columns
    sizes = (tile_dev, shifts, terms // shifts, tile_rows, total)
    piece_rows = rows + STAT_ROWS
    lookup = source_tile_lookup
    own_records = lax.dynamic_slice_in_dim(lookup, own * tile_dev, tile_dev, 0).reshape(records)
    source = own_records // tile_dev
    local = own_records % tile_dev
    devices = jnp.arange(peers, dtype=jnp.int32)
    use_ring = peers * tile_dev <= 2 * records

    if use_ring:
        chips = peers // 2
        onward = ring_pairs(peers)
        sibling = [(i, i ^ 1) for i in range(peers)]
        core = own % 2
        here = ring_place(own // 2, chips)

        half = chips // 2
        groups = [[(0, 0, 0), (0, 0, 1)]]
        for step in range(1, half):
            groups += [[(step, shard, 0), (step, shard, 1)] for shard in (0, 1)]
        groups += [[(half, 0, 0), (half, 0, 1)]]
        slots = [
            (p, j * piece_rows + rows) for p, group in enumerate(groups) for j in range(len(group))
        ]
        firsts = [sum(len(group) for group in groups[:p]) for p in range(1, len(groups))]
        codes = [(4 * step + 2 * shard + swap) for group in groups for step, shard, swap in group]

        def code_of(device):
            ahead = (here - ring_place(device // 2, chips)) % chips
            steps = jnp.where(core == 0, ahead, (chips - ahead) % chips)
            other = (device + core) % 2
            direct = 4 * steps + 2 * other
            swapped = 4 * (chips - steps) + 2 * (1 - other) + 1
            code = jnp.where(steps < half, direct, swapped)
            code = jnp.where(steps == half, 4 * half + other, code)
            return jnp.where(steps == 0, other, code)

        def slot_of(device):
            same = code_of(device)[:, None] == jnp.array(codes, jnp.int32)[None, :]
            return jnp.sum(same * jnp.arange(len(codes), dtype=jnp.int32), axis=1)

        record_slot = slot_of(source)
        phase = sum((record_slot >= slot).astype(jnp.int32) for slot in firsts)
        first_slot = sum((phase == p + 1) * slot for p, slot in enumerate(firsts))
        offset = (record_slot - first_slot) * piece_rows + local * tile_rows
        stat_offset = slot_of(devices) * STAT_ROWS

        def swap_cores(x):
            return lax.ppermute(x, "sector", sibling)

        def step_on(x):
            return lax.ppermute(x, "sector", onward)

        def exchange(piece, contract, prepare, late=False):
            first, second = lax.optimization_barrier((piece, swap_cores(piece)))
            pairs = [(first, second)]
            for step in range(1, half):
                first = step_on(first)
                pairs.append((first, swap_cores(first)))
                second = step_on(second)
                pairs.append((second, swap_cores(second)))
            near = prepare(pairs[0][1])
            first = step_on(first)
            buffers = [jnp.concatenate(pair, axis=0) for pair in pairs]
            left = []
            order = list(range(len(buffers)))
            if late:
                order = order[1:3] + order[:1] + order[3:]
            for p in order:
                left = [contract(p, buffers[p], near, left)]
                if p == len(buffers) - 2:
                    first, left[0] = lax.optimization_barrier((first, left[0]))
            buffers.append(jnp.concatenate([first, swap_cores(first)], axis=0))
            left = [contract(len(pairs), buffers[-1], near, left)]
            return buffers, near, left[0]

    else:
        capacity = max(1, 2 * records // peers)
        is_self = source == own
        hot = ((source[:, None] == devices[None, :]) & ~is_self[:, None]).astype(jnp.int32)
        rank = jnp.sum(hot * jnp.cumsum(hot, axis=0), axis=1) - 1
        every = lookup.reshape(peers, records)
        wanted = ((every // tile_dev == own) & (devices != own)[:, None]).astype(jnp.int32)
        order = jnp.cumsum(wanted, axis=1) - 1
        slots = jnp.arange(capacity, dtype=jnp.int32)
        chosen = wanted[:, :, None] * (order[:, :, None] == slots).astype(jnp.int32)
        send_index = jnp.sum(chosen * (every % tile_dev)[:, :, None], axis=1).reshape(-1)
        place = jnp.where(is_self, local, tile_dev + source * capacity + rank)
        phase = jnp.zeros_like(source)
        offset = place * tile_rows
        stat_offset = devices * STAT_ROWS
        stat_base = (tile_dev + peers * capacity) * tile_rows
        slots = [(0, stat_base + d * STAT_ROWS) for d in range(peers)]

        def exchange(piece, contract, prepare, late=False):
            tiles = piece[:rows].reshape(tile_dev, tile_rows, columns)
            incoming = lax.all_to_all(tiles[send_index], "sector", 0, 0, tiled=True)
            stats = lax.all_gather(piece[rows:], "sector", axis=0, tiled=True)
            buffer = jnp.concatenate([piece[:rows], incoming.reshape(-1, columns), stats], axis=0)
            near = prepare(piece)
            return [buffer], near, contract(0, buffer, near, [])

    vmem = pl.BlockSpec(memory_space=pltpu.VMEM)
    smem = pl.BlockSpec(memory_space=pltpu.SMEM)
    hbm = pl.BlockSpec(memory_space=pltpu.HBM)

    piece = pl.pallas_call(
        start_kernel,
        out_shape=jax.ShapeDtypeStruct((piece_rows, columns), bf16),
        in_specs=[vmem],
        out_specs=vmem,
        compiler_params=pltpu.CompilerParams(vmem_limit_bytes=4 * 2**20),
    )(wavefunction)
    phases = max(p for p, _ in slots) + 1
    env_flat = env_left.reshape(tile_dev * terms * tile_rows, tile_rows)
    right_flat = right_environment_terms.reshape(terms * columns, columns)
    left_type = pltpu.VMEM((shifts * rows, (terms // shifts) * columns), bf16)

    def prepare(marker):
        tied = lax.optimization_barrier((phase, offset, env_flat, marker))
        counts, lists, env_near = pl.pallas_call(
            functools.partial(prepare_kernel, sizes, phases),
            out_shape=(
                jax.ShapeDtypeStruct((phases,), jnp.int32),
                jax.ShapeDtypeStruct((3, phases * records), jnp.int32),
                pltpu.VMEM(env_flat.shape, bf16),
            ),
            in_specs=[smem, smem, hbm],
            out_specs=(smem, smem, vmem),
            scratch_shapes=[pltpu.SemaphoreType.DMA((LOADS,))],
            compiler_params=pltpu.CompilerParams(vmem_limit_bytes=40 * 2**20),
        )(*tied[:3])
        return env_near, right_flat, counts, lists

    def contract(phase, buffer, near, held):
        env_near, right_near, counts, lists = near
        return pl.pallas_call(
            functools.partial(left_kernel, phase, 8 if phase == 0 else 10, sizes),
            out_shape=left_type,
            in_specs=[smem, smem] + [vmem] * (2 + len(held)),
            out_specs=vmem,
            input_output_aliases={4: 0} if held else {},
            compiler_params=pltpu.CompilerParams(vmem_limit_bytes=4 * 2**20),
            cost_estimate=pl.CostEstimate(flops=2**30, bytes_accessed=2**20, transcendentals=0),
        )(counts, lists, buffer, env_near, *held)

    def apply_operator(stage, buffers, near, held, prior, coefs):
        image = jax.ShapeDtypeStruct((rows, columns), f32)
        small = jax.ShapeDtypeStruct((8, 128), f32)
        send = small if stage == 3 else jax.ShapeDtypeStruct((piece_rows, columns), bf16)
        env_near, right_near, counts, lists = near
        operands = [right_near, wavefunction, *buffers, *prior, *coefs, held]
        return pl.pallas_call(
            functools.partial(apply_kernel, stage, sizes, slots),
            out_shape=(image, small, send),
            in_specs=[smem] + [vmem] * len(operands),
            out_specs=(vmem, vmem, vmem),
            scratch_shapes=[pltpu.VMEM((peers * STAT_ROWS, 128), bf16)],
            compiler_params=pltpu.CompilerParams(vmem_limit_bytes=12 * 2**20),
            cost_estimate=pl.CostEstimate(
                flops=4 * rows * terms * tile_rows * columns, bytes_accessed=2**24, transcendentals=0
            ),
        )(stat_offset, *operands)

    buffers, near, held = exchange(piece, contract, prepare, True)
    image_one, coefs_one, piece = apply_operator(1, buffers, near, held, [], [])

    def prepared(marker):
        return near

    buffers, _, held = exchange(piece, contract, prepared)
    image_two, coefs_two, piece = apply_operator(2, buffers, near, held, [image_one], [coefs_one])
    buffers, _, held = exchange(piece, contract, prepared)
    image_three, coefs_three, stats = apply_operator(
        3, buffers, near, held, [image_one, image_two], [coefs_two]
    )
    distance = 1
    while distance < peers:
        pairs = [(i, i ^ distance) for i in range(peers)]
        stats = stats + lax.ppermute(stats, "sector", pairs)
        distance *= 2
    projected = pl.pallas_call(
        functools.partial(finish_kernel, total),
        out_shape=jax.ShapeDtypeStruct((3, 3), f32),
        in_specs=[vmem, vmem],
        out_specs=vmem,
        compiler_params=pltpu.CompilerParams(vmem_limit_bytes=2 * 2**20),
    )(stats, coefs_three)
    return (image_three, projected)


def solution(mesh):
    return jax.shard_map(
        per_device,
        mesh=mesh,
        in_specs=(
            P(("groups", "sector"), None),
            P(("groups", "sector"), None, None, None),
            P("groups", None, None),
            P("groups", None),
        ),
        out_specs=(P(("groups", "sector"), None), P("groups", None)),
        check_vma=False,
    )
```

```python
import functools

import jax
import jax.numpy as jnp
from jax import lax
from jax.experimental import pallas as pl
from jax.experimental.pallas import tpu as pltpu
from jax.sharding import PartitionSpec as P

epsilon = 1e-06
f32 = jnp.float32
bf16 = jnp.bfloat16
STAT_ROWS = 16
LOADS = 4


def row(value):
    return jnp.broadcast_to(value, (1, 128))


def lane_sums(product):
    return jnp.sum(product, axis=0, keepdims=True)


def split_rows(sums):
    rows = []
    for value in sums:
        high = value.astype(bf16)
        rest = value - high.astype(f32)
        middle = rest.astype(bf16)
        low = (rest - middle.astype(f32)).astype(bf16)
        rows += [high, middle, low]
    rows += [jnp.zeros((1, 128), bf16)] * (STAT_ROWS - len(rows))
    return jnp.concatenate([r.astype(f32) for r in rows], axis=0).astype(bf16)


def start_kernel(w_ref, piece_ref):
    rows = w_ref.shape[0]
    w = w_ref[...]
    piece_ref[0:rows, :] = w
    wide = w.astype(f32)
    piece_ref[rows:, :] = split_rows([lane_sums(wide * wide)])


def prepare_kernel(sizes, phases, phase_ref, offset_ref, place_ref, env_ref, *rest):
    count_ref, list_ref, stat_ref, env_out, sems = rest
    tile_dev, shifts, group, tile_rows, total = sizes
    records = tile_dev * shifts
    step = env_ref.shape[0] // LOADS
    copies = []
    for j in range(LOADS):
        rows = pl.ds(j * step, step)
        copies.append(pltpu.make_async_copy(env_ref.at[rows], env_out.at[rows], sems.at[j]))
    for copy in copies:
        copy.start()
    for p in range(phases):
        count_ref[p] = 0

    def one_tile(tile, carry):
        for shift in range(shifts):
            r = tile * shifts + shift
            p = phase_ref[r]
            n = count_ref[p]
            list_ref[0, p * records + n] = offset_ref[r]
            list_ref[1, p * records + n] = r * group * tile_rows
            list_ref[2, p * records + n] = (shift * tile_dev + tile) * tile_rows
            count_ref[p] = n + 1
        return carry

    def one_place(d, carry):
        stat_ref[d] = place_ref[d]
        return carry

    lax.fori_loop(0, tile_dev, one_tile, 0)
    lax.fori_loop(0, place_ref.shape[0], one_place, 0)
    for copy in copies:
        copy.wait()


def contract_left(phase, unroll, sizes, count_ref, list_ref, buf_ref, env_ref, left_ref):
    tile_dev, shifts, group, tile_rows, total = sizes
    base = phase * tile_dev * shifts
    width = group * tile_rows
    count = count_ref[phase]

    def one(n):
        offset = pl.multiple_of(list_ref[0, n], 16)
        start = pl.multiple_of(list_ref[1, n], 128)
        target = pl.multiple_of(list_ref[2, n], 128)
        picked = buf_ref[pl.ds(offset, tile_rows), :]
        for t in range(group):
            left_ref[pl.ds(target, tile_rows), t * 128 : (t + 1) * 128] = jnp.dot(
                env_ref[pl.ds(start + t * tile_rows, tile_rows), :],
                picked,
                preferred_element_type=f32,
            ).astype(bf16)

    def many(j, carry):
        for q in range(unroll):
            one(base + j * unroll + q)
        return carry

    def few(j, carry):
        for q in range(4):
            one(base + jnp.minimum(whole * unroll + j * 4 + q, count - 1))
        return carry

    whole = count // unroll
    lax.fori_loop(0, whole, many, 0)
    lax.fori_loop(0, (count - whole * unroll + 3) // 4, few, 0)


def left_kernel(phase, unroll, sizes, count_ref, list_ref, buf_ref, env_ref, *rest):
    contract_left(phase, unroll, sizes, count_ref, list_ref, buf_ref, env_ref, rest[-1])


def apply_kernel(stage, sizes, slots, stat_ref, right_ref, w_ref, *rest):
    tile_dev, shifts, group, tile_rows, total = sizes
    rows = tile_dev * tile_rows
    phases = max(p for p, _ in slots) + 1
    bufs, rest = rest[:phases], rest[phases:]
    prior, rest = rest[: stage - 1], rest[stage - 1 :]
    if stage > 1:
        coef_in, rest = rest[0], rest[1:]
    left_ref, image_ref, coef_ref, send_ref, all_stats = rest

    width = group * tile_rows
    applied = jnp.zeros((rows, 128), f32)
    for k in range(shifts):
        applied = applied + jnp.dot(
            left_ref[k * rows : (k + 1) * rows, :],
            right_ref[k * width : (k + 1) * width, :],
            preferred_element_type=f32,
        )

    for n, (p, offset) in enumerate(slots):
        all_stats[n * STAT_ROWS : (n + 1) * STAT_ROWS, :] = bufs[p][offset : offset + STAT_ROWS, :]
    gathered = jnp.zeros((STAT_ROWS, 128), f32)
    for d in range(stat_ref.shape[0]):
        offset = pl.multiple_of(stat_ref[d], 16)
        gathered = gathered + all_stats[pl.ds(offset, STAT_ROWS), :].astype(f32)

    def mean_of(j):
        lanes = gathered[3 * j : 3 * j + 1] + gathered[3 * j + 1 : 3 * j + 2]
        lanes = lanes + gathered[3 * j + 2 : 3 * j + 3]
        return row(jnp.sum(lanes, axis=1, keepdims=True) * (1.0 / total))

    w = w_ref[...].astype(f32)
    if stage == 1:
        square = mean_of(0)
        scale = lax.rsqrt(square + epsilon)
        coefs = [scale, scale * scale * square]
        image = scale * applied
        sums = [lane_sums((w * scale) * image), lane_sums(image * image)]
    elif stage == 2:
        scale, g11 = coef_in[0:1, :], coef_in[1:2, :]
        aa, norm = mean_of(0), mean_of(1)
        rest_square = jnp.maximum(norm - 2.0 * aa * aa + aa * aa * g11, 0.0)
        ba = jnp.sqrt(rest_square + epsilon)
        g12 = (aa - aa * g11) / ba
        g22 = rest_square / (ba * ba)
        coefs = [scale, g11, aa, ba, g12, g22]
        first = prior[0][...]
        basis_one = w * scale
        basis_two = (first - aa * basis_one) / ba
        image = (applied - aa * first) / ba
        sums = [
            lane_sums(basis_one * image),
            lane_sums(basis_two * image),
            lane_sums(image * image),
        ]
    else:
        scale, g11, aa, ba, g12, g22 = [coef_in[j : j + 1, :] for j in range(6)]
        ab, bb, norm = mean_of(0), mean_of(1), mean_of(2)
        rest_square = norm - 2.0 * (ab * ab + bb * bb) + ab * ab * g11 + bb * bb * g22
        rest_square = jnp.maximum(rest_square + 2.0 * ab * bb * g12, 0.0)
        cb = jnp.sqrt(rest_square + epsilon)
        coefs = [aa, ab, ba, bb, cb]
        first, second = prior[0][...], prior[1][...]
        basis_one = w * scale
        basis_two = (first - aa * basis_one) / ba
        basis_three = (second - ab * basis_one - bb * basis_two) / cb
        image = (applied - ab * first - bb * second) / cb
        sums = [lane_sums(b * image) for b in (basis_one, basis_two, basis_three)]

    image_ref[...] = image
    coef_ref[...] = jnp.concatenate(coefs + [jnp.zeros((1, 128), f32)] * (8 - len(coefs)), axis=0)
    if stage < 3:
        rows = image.shape[0]
        send_ref[0:rows, :] = image.astype(bf16)
        send_ref[rows:, :] = split_rows(sums)
    else:
        send_ref[...] = jnp.concatenate(sums + [jnp.zeros((1, 128), f32)] * 5, axis=0)


def finish_kernel(total, stat_ref, coef_ref, out_ref):
    last = [row(jnp.sum(stat_ref[j : j + 1, :], axis=1, keepdims=True) * (1.0 / total)) for j in range(3)]
    aa, ab, ba, bb, cb = [coef_ref[j : j + 1, :] for j in range(5)]
    lane = lax.broadcasted_iota(jnp.int32, (1, 128), 1)

    def line(a, b, c):
        return jnp.where(lane == 0, a, jnp.where(lane == 1, b, c))

    zero = jnp.zeros((1, 128), f32)
    table = jnp.concatenate(
        [line(aa, ab, last[0]), line(ba, bb, last[1]), line(zero, cb, last[2])], axis=0
    )
    out_ref[...] = table[:, 0:3]


def ring_pairs(peers):
    chips = peers // 2
    order = list(range(0, chips, 2)) + list(range(chips - 1, 0, -2))
    pairs = []
    for j in range(chips):
        here, after = order[j] * 2, order[(j + 1) % chips] * 2
        pairs += [(here, after), (after + 1, here + 1)]
    return pairs


def ring_place(chip, chips):
    return jnp.where(chip % 2 == 0, chip // 2, chips - 1 - chip // 2)


def per_device(wavefunction, env_left, right_environment_terms, source_tile_lookup):
    peers = lax.axis_size("sector")
    own = lax.axis_index("sector")
    tile_dev, terms, tile_rows = env_left.shape[0], env_left.shape[1], env_left.shape[2]
    rows, columns = wavefunction.shape
    shifts = source_tile_lookup.shape[1]
    records = tile_dev * shifts
    total = peers * rows * columns
    sizes = (tile_dev, shifts, terms // shifts, tile_rows, total)
    piece_rows = rows + STAT_ROWS
    lookup = source_tile_lookup
    own_records = lax.dynamic_slice_in_dim(lookup, own * tile_dev, tile_dev, 0).reshape(records)
    source = own_records // tile_dev
    local = own_records % tile_dev
    devices = jnp.arange(peers, dtype=jnp.int32)
    use_ring = peers * tile_dev <= 2 * records

    if use_ring:
        chips = peers // 2
        onward = ring_pairs(peers)
        sibling = [(i, i ^ 1) for i in range(peers)]
        core = own % 2
        here = ring_place(own // 2, chips)

        half = chips // 2
        groups = [[(0, 0, 0), (0, 0, 1)]]
        for step in range(1, half):
            groups += [[(step, shard, 0), (step, shard, 1)] for shard in (0, 1)]
        groups += [[(half, 0, 0), (half, 0, 1)]]
        slots = [
            (p, j * piece_rows + rows) for p, group in enumerate(groups) for j in range(len(group))
        ]
        firsts = [sum(len(group) for group in groups[:p]) for p in range(1, len(groups))]
        codes = [(4 * step + 2 * shard + swap) for group in groups for step, shard, swap in group]

        def code_of(device):
            ahead = (here - ring_place(device // 2, chips)) % chips
            steps = jnp.where(core == 0, ahead, (chips - ahead) % chips)
            other = (device + core) % 2
            direct = 4 * steps + 2 * other
            swapped = 4 * (chips - steps) + 2 * (1 - other) + 1
            code = jnp.where(steps < half, direct, swapped)
            code = jnp.where(steps == half, 4 * half + other, code)
            return jnp.where(steps == 0, other, code)

        def slot_of(device):
            same = code_of(device)[:, None] == jnp.array(codes, jnp.int32)[None, :]
            return jnp.sum(same * jnp.arange(len(codes), dtype=jnp.int32), axis=1)

        record_slot = slot_of(source)
        phase = sum((record_slot >= slot).astype(jnp.int32) for slot in firsts)
        first_slot = sum((phase == p + 1) * slot for p, slot in enumerate(firsts))
        offset = (record_slot - first_slot) * piece_rows + local * tile_rows
        stat_offset = slot_of(devices) * STAT_ROWS

        def swap_cores(x):
            return lax.ppermute(x, "sector", sibling)

        def step_on(x):
            return lax.ppermute(x, "sector", onward)

        def exchange(piece, contract, prepare, late=False):
            first, second = lax.optimization_barrier((piece, swap_cores(piece)))
            pairs = [(first, second)]
            for step in range(1, half):
                first = step_on(first)
                pairs.append((first, swap_cores(first)))
                second = step_on(second)
                pairs.append((second, swap_cores(second)))
            near = prepare(pairs[0][1])
            first = step_on(first)
            buffers = [jnp.concatenate(pair, axis=0) for pair in pairs]
            left = []
            order = list(range(len(buffers)))
            if late:
                order = order[1:3] + order[:1] + order[3:]
            for p in order:
                left = [contract(p, buffers[p], near, left)]
                if p == len(buffers) - 2:
                    first, left[0] = lax.optimization_barrier((first, left[0]))
            buffers.append(jnp.concatenate([first, swap_cores(first)], axis=0))
            left = [contract(len(pairs), buffers[-1], near, left)]
            return buffers, near, left[0]

    else:
        capacity = max(1, 2 * records // peers)
        is_self = source == own
        hot = ((source[:, None] == devices[None, :]) & ~is_self[:, None]).astype(jnp.int32)
        rank = jnp.sum(hot * jnp.cumsum(hot, axis=0), axis=1) - 1
        every = lookup.reshape(peers, records)
        wanted = ((every // tile_dev == own) & (devices != own)[:, None]).astype(jnp.int32)
        order = jnp.cumsum(wanted, axis=1) - 1
        slots = jnp.arange(capacity, dtype=jnp.int32)
        chosen = wanted[:, :, None] * (order[:, :, None] == slots).astype(jnp.int32)
        send_index = jnp.sum(chosen * (every % tile_dev)[:, :, None], axis=1).reshape(-1)
        place = jnp.where(is_self, local, tile_dev + source * capacity + rank)
        phase = jnp.zeros_like(source)
        offset = place * tile_rows
        stat_offset = devices * STAT_ROWS
        stat_base = (tile_dev + peers * capacity) * tile_rows
        slots = [(0, stat_base + d * STAT_ROWS) for d in range(peers)]

        def exchange(piece, contract, prepare, late=False):
            tiles = piece[:rows].reshape(tile_dev, tile_rows, columns)
            incoming = lax.all_to_all(tiles[send_index], "sector", 0, 0, tiled=True)
            stats = lax.all_gather(piece[rows:], "sector", axis=0, tiled=True)
            buffer = jnp.concatenate([piece[:rows], incoming.reshape(-1, columns), stats], axis=0)
            near = prepare(piece)
            return [buffer], near, contract(0, buffer, near, [])

    vmem = pl.BlockSpec(memory_space=pltpu.VMEM)
    smem = pl.BlockSpec(memory_space=pltpu.SMEM)
    hbm = pl.BlockSpec(memory_space=pltpu.HBM)

    piece = pl.pallas_call(
        start_kernel,
        out_shape=jax.ShapeDtypeStruct((piece_rows, columns), bf16),
        in_specs=[vmem],
        out_specs=vmem,
        compiler_params=pltpu.CompilerParams(vmem_limit_bytes=4 * 2**20),
    )(wavefunction)
    phases = max(p for p, _ in slots) + 1
    env_flat = env_left.reshape(tile_dev * terms * tile_rows, tile_rows)
    right_flat = right_environment_terms.reshape(terms * columns, columns)
    left_type = pltpu.VMEM((shifts * rows, (terms // shifts) * columns), bf16)

    def prepare(marker):
        tied = lax.optimization_barrier((phase, offset, stat_offset, env_flat, marker))
        counts, lists, places, env_near = pl.pallas_call(
            functools.partial(prepare_kernel, sizes, phases),
            out_shape=(
                pltpu.SMEM((phases,), jnp.int32),
                pltpu.SMEM((3, phases * records), jnp.int32),
                pltpu.SMEM((peers,), jnp.int32),
                pltpu.VMEM(env_flat.shape, bf16),
            ),
            in_specs=[smem, smem, smem, hbm],
            out_specs=(smem, smem, smem, vmem),
            scratch_shapes=[pltpu.SemaphoreType.DMA((LOADS,))],
            compiler_params=pltpu.CompilerParams(vmem_limit_bytes=40 * 2**20),
        )(*tied[:4])
        return env_near, right_flat, counts, lists, places

    def contract(phase, buffer, near, held):
        env_near, right_near, counts, lists, places = near
        return pl.pallas_call(
            functools.partial(left_kernel, phase, 8 if phase == 0 else 10, sizes),
            out_shape=left_type,
            in_specs=[smem, smem] + [vmem] * (2 + len(held)),
            out_specs=vmem,
            input_output_aliases={4: 0} if held else {},
            compiler_params=pltpu.CompilerParams(vmem_limit_bytes=4 * 2**20),
            cost_estimate=pl.CostEstimate(flops=2**30, bytes_accessed=2**20, transcendentals=0),
        )(counts, lists, buffer, env_near, *held)

    def apply_operator(stage, buffers, near, held, prior, coefs):
        image = pltpu.VMEM((rows, columns), f32)
        small = jax.ShapeDtypeStruct((8, 128), f32)
        send = small if stage == 3 else jax.ShapeDtypeStruct((piece_rows, columns), bf16)
        env_near, right_near, counts, lists, places = near
        operands = [right_near, wavefunction, *buffers, *prior, *coefs, held]
        return pl.pallas_call(
            functools.partial(apply_kernel, stage, sizes, slots),
            out_shape=(image, small, send),
            in_specs=[smem] + [vmem] * len(operands),
            out_specs=(vmem, vmem, vmem),
            scratch_shapes=[pltpu.VMEM((peers * STAT_ROWS, 128), bf16)],
            compiler_params=pltpu.CompilerParams(vmem_limit_bytes=12 * 2**20),
            cost_estimate=pl.CostEstimate(
                flops=4 * rows * terms * tile_rows * columns, bytes_accessed=2**24, transcendentals=0
            ),
        )(places, *operands)

    buffers, near, held = exchange(piece, contract, prepare, True)
    image_one, coefs_one, piece = apply_operator(1, buffers, near, held, [], [])

    def prepared(marker):
        return near

    buffers, _, held = exchange(piece, contract, prepared)
    image_two, coefs_two, piece = apply_operator(2, buffers, near, held, [image_one], [coefs_one])
    buffers, _, held = exchange(piece, contract, prepared)
    image_three, coefs_three, stats = apply_operator(
        3, buffers, near, held, [image_one, image_two], [coefs_two]
    )
    distance = 1
    while distance < peers:
        pairs = [(i, i ^ distance) for i in range(peers)]
        stats = stats + lax.ppermute(stats, "sector", pairs)
        distance *= 2
    projected = pl.pallas_call(
        functools.partial(finish_kernel, total),
        out_shape=jax.ShapeDtypeStruct((3, 3), f32),
        in_specs=[vmem, vmem],
        out_specs=vmem,
        compiler_params=pltpu.CompilerParams(vmem_limit_bytes=2 * 2**20),
    )(stats, coefs_three)
    return (image_three, projected)


def solution(mesh):
    return jax.shard_map(
        per_device,
        mesh=mesh,
        in_specs=(
            P(("groups", "sector"), None),
            P(("groups", "sector"), None, None, None),
            P("groups", None, None),
            P("groups", None),
        ),
        out_specs=(P(("groups", "sector"), None), P("groups", None)),
        check_vma=False,
    )
```

```python
import functools

import jax
import jax.numpy as jnp
from jax import lax
from jax.experimental import pallas as pl
from jax.experimental.pallas import tpu as pltpu
from jax.sharding import PartitionSpec as P

epsilon = 1e-06
f32 = jnp.float32
bf16 = jnp.bfloat16
STAT_ROWS = 16
LOADS = 4


def row(value):
    return jnp.broadcast_to(value, (1, 128))


def lane_sums(product):
    return jnp.sum(product, axis=0, keepdims=True)


def split_rows(sums):
    rows = []
    for value in sums:
        high = value.astype(bf16)
        rest = value - high.astype(f32)
        middle = rest.astype(bf16)
        low = (rest - middle.astype(f32)).astype(bf16)
        rows += [high, middle, low]
    rows += [jnp.zeros((1, 128), bf16)] * (STAT_ROWS - len(rows))
    return jnp.concatenate([r.astype(f32) for r in rows], axis=0).astype(bf16)


def start_kernel(w_ref, piece_ref):
    rows = w_ref.shape[0]
    w = w_ref[...]
    piece_ref[0:rows, :] = w
    wide = w.astype(f32)
    piece_ref[rows:, :] = split_rows([lane_sums(wide * wide)])


def ring_place(chip, chips):
    return jnp.where(chip % 2 == 0, chip // 2, chips - 1 - chip // 2)


def prepare_kernel(sizes, phases, peers, ring, own_ref, first_ref, second_ref, env_ref, *rest):
    count_ref, list_ref, stat_ref, env_out, first, second, sems = rest
    tile_dev, shifts, group, tile_rows, total = sizes
    records = tile_dev * shifts
    large = pltpu.make_async_copy(env_ref, env_out, sems.at[0])
    large.start()
    small = [
        pltpu.make_async_copy(first_ref, first, sems.at[1]),
        pltpu.make_async_copy(second_ref, second, sems.at[2]),
    ]
    for copy in small:
        copy.start()
    for p in range(phases):
        count_ref[p] = 0

    if ring:
        own = own_ref[0]
        core = own % 2
        chips = peers // 2
        here = ring_place(own // 2, chips)
        for d in range(peers):
            ahead = here - (d // 4 if d // 2 % 2 == 0 else chips - 1 - d // 4)
            ahead = jnp.where(ahead < 0, ahead + chips, ahead)
            steps = jnp.where(core == 0, ahead, jnp.where(ahead == 0, 0, chips - ahead))
            other = core if d % 2 == 0 else 1 - core
            slot = jnp.where(
                steps < chips // 2, 4 * steps - 2 + 2 * other, 4 * (chips - steps) + 1 - 2 * other
            )
            slot = jnp.where(steps == chips // 2, 2 * chips - 2 + other, slot)
            stat_ref[d] = jnp.where(steps == 0, other, slot) * STAT_ROWS
    else:

        def one_place(d, carry):
            stat_ref[d] = d * STAT_ROWS
            return carry

        lax.fori_loop(0, peers, one_place, 0)
    for copy in small:
        copy.wait()

    def one_tile(tile, carry):
        for shift in range(shifts):
            r = tile * shifts + shift
            if ring:
                source = first[r]
                device = lax.div(source, tile_dev)
                p = lax.div(stat_ref[device], STAT_ROWS)
                offset = (source - device * tile_dev) * tile_rows
            else:
                p, offset = first[r], second[r]
            n = count_ref[p]
            list_ref[0, p * records + n] = offset
            list_ref[1, p * records + n] = r * group * tile_rows
            list_ref[2, p * records + n] = (shift * tile_dev + tile) * tile_rows
            count_ref[p] = n + 1
        return carry

    lax.fori_loop(0, tile_dev, one_tile, 0)
    large.wait()


def contract_left(phase, unroll, sizes, count_ref, list_ref, buf_ref, env_ref, left_ref):
    tile_dev, shifts, group, tile_rows, total = sizes
    base = phase * tile_dev * shifts
    width = group * tile_rows
    count = count_ref[phase]

    def one(n):
        offset = pl.multiple_of(list_ref[0, n], 16)
        start = pl.multiple_of(list_ref[1, n], 128)
        target = pl.multiple_of(list_ref[2, n], 128)
        picked = buf_ref[pl.ds(offset, tile_rows), :]
        for t in range(group):
            left_ref[pl.ds(target, tile_rows), t * 128 : (t + 1) * 128] = jnp.dot(
                env_ref[pl.ds(start + t * tile_rows, tile_rows), :],
                picked,
                preferred_element_type=f32,
            ).astype(bf16)

    def many(j, carry):
        for q in range(unroll):
            one(base + j * unroll + q)
        return carry

    def few(j, carry):
        for q in range(4):
            one(base + jnp.minimum(whole * unroll + j * 4 + q, count - 1))
        return carry

    whole = count // unroll
    lax.fori_loop(0, whole, many, 0)
    lax.fori_loop(0, (count - whole * unroll + 3) // 4, few, 0)


def left_kernel(phase, unroll, sizes, count_ref, list_ref, buf_ref, env_ref, *rest):
    contract_left(phase, unroll, sizes, count_ref, list_ref, buf_ref, env_ref, rest[-1])


def apply_kernel(stage, sizes, slots, stat_ref, right_ref, w_ref, *rest):
    tile_dev, shifts, group, tile_rows, total = sizes
    rows = tile_dev * tile_rows
    phases = max(p for p, _ in slots) + 1
    bufs, rest = rest[:phases], rest[phases:]
    prior, rest = rest[: stage - 1], rest[stage - 1 :]
    if stage > 1:
        coef_in, rest = rest[0], rest[1:]
    left_ref, image_ref, coef_ref, send_ref, all_stats = rest

    width = group * tile_rows
    applied = jnp.zeros((rows, 128), f32)
    for k in range(shifts):
        applied = applied + jnp.dot(
            left_ref[k * rows : (k + 1) * rows, :],
            right_ref[k * width : (k + 1) * width, :],
            preferred_element_type=f32,
        )

    for n, (p, offset) in enumerate(slots):
        all_stats[n * STAT_ROWS : (n + 1) * STAT_ROWS, :] = bufs[p][offset : offset + STAT_ROWS, :]
    gathered = jnp.zeros((STAT_ROWS, 128), f32)
    for d in range(stat_ref.shape[0]):
        offset = pl.multiple_of(stat_ref[d], 16)
        gathered = gathered + all_stats[pl.ds(offset, STAT_ROWS), :].astype(f32)

    def mean_of(j):
        lanes = gathered[3 * j : 3 * j + 1] + gathered[3 * j + 1 : 3 * j + 2]
        lanes = lanes + gathered[3 * j + 2 : 3 * j + 3]
        return row(jnp.sum(lanes, axis=1, keepdims=True) * (1.0 / total))

    w = w_ref[...].astype(f32)
    if stage == 1:
        square = mean_of(0)
        scale = lax.rsqrt(square + epsilon)
        coefs = [scale, scale * scale * square]
        image = scale * applied
        sums = [lane_sums((w * scale) * image), lane_sums(image * image)]
    elif stage == 2:
        scale, g11 = coef_in[0:1, :], coef_in[1:2, :]
        aa, norm = mean_of(0), mean_of(1)
        rest_square = jnp.maximum(norm - 2.0 * aa * aa + aa * aa * g11, 0.0)
        ba = jnp.sqrt(rest_square + epsilon)
        g12 = (aa - aa * g11) / ba
        g22 = rest_square / (ba * ba)
        coefs = [scale, g11, aa, ba, g12, g22]
        first = prior[0][...]
        basis_one = w * scale
        basis_two = (first - aa * basis_one) / ba
        image = (applied - aa * first) / ba
        sums = [
            lane_sums(basis_one * image),
            lane_sums(basis_two * image),
            lane_sums(image * image),
        ]
    else:
        scale, g11, aa, ba, g12, g22 = [coef_in[j : j + 1, :] for j in range(6)]
        ab, bb, norm = mean_of(0), mean_of(1), mean_of(2)
        rest_square = norm - 2.0 * (ab * ab + bb * bb) + ab * ab * g11 + bb * bb * g22
        rest_square = jnp.maximum(rest_square + 2.0 * ab * bb * g12, 0.0)
        cb = jnp.sqrt(rest_square + epsilon)
        coefs = [aa, ab, ba, bb, cb]
        first, second = prior[0][...], prior[1][...]
        basis_one = w * scale
        basis_two = (first - aa * basis_one) / ba
        basis_three = (second - ab * basis_one - bb * basis_two) / cb
        image = (applied - ab * first - bb * second) / cb
        sums = [lane_sums(b * image) for b in (basis_one, basis_two, basis_three)]

    image_ref[...] = image
    coef_ref[...] = jnp.concatenate(coefs + [jnp.zeros((1, 128), f32)] * (8 - len(coefs)), axis=0)
    if stage < 3:
        rows = image.shape[0]
        send_ref[0:rows, :] = image.astype(bf16)
        send_ref[rows:, :] = split_rows(sums)
    else:
        send_ref[...] = jnp.concatenate(sums + [jnp.zeros((1, 128), f32)] * 5, axis=0)


def finish_kernel(total, stat_ref, coef_ref, out_ref):
    last = [row(jnp.sum(stat_ref[j : j + 1, :], axis=1, keepdims=True) * (1.0 / total)) for j in range(3)]
    aa, ab, ba, bb, cb = [coef_ref[j : j + 1, :] for j in range(5)]
    lane = lax.broadcasted_iota(jnp.int32, (1, 128), 1)

    def line(a, b, c):
        return jnp.where(lane == 0, a, jnp.where(lane == 1, b, c))

    zero = jnp.zeros((1, 128), f32)
    table = jnp.concatenate(
        [line(aa, ab, last[0]), line(ba, bb, last[1]), line(zero, cb, last[2])], axis=0
    )
    out_ref[...] = table[:, 0:3]


def ring_pairs(peers):
    chips = peers // 2
    order = list(range(0, chips, 2)) + list(range(chips - 1, 0, -2))
    pairs = []
    for j in range(chips):
        here, after = order[j] * 2, order[(j + 1) % chips] * 2
        pairs += [(here, after), (after + 1, here + 1)]
    return pairs


def per_device(wavefunction, env_left, right_environment_terms, source_tile_lookup):
    peers = lax.axis_size("sector")
    own = lax.axis_index("sector")
    tile_dev, terms, tile_rows = env_left.shape[0], env_left.shape[1], env_left.shape[2]
    rows, columns = wavefunction.shape
    shifts = source_tile_lookup.shape[1]
    records = tile_dev * shifts
    total = peers * rows * columns
    sizes = (tile_dev, shifts, terms // shifts, tile_rows, total)
    piece_rows = rows + STAT_ROWS
    lookup = source_tile_lookup
    own_records = lax.dynamic_slice_in_dim(lookup, own * tile_dev, tile_dev, 0).reshape(records)
    devices = jnp.arange(peers, dtype=jnp.int32)
    use_ring = peers * tile_dev <= 2 * records

    if use_ring:
        chips = peers // 2
        onward = ring_pairs(peers)
        sibling = [(i, i ^ 1) for i in range(peers)]
        half = chips // 2
        slots = [(p, rows) for p in range(peers)]
        first_list = second_list = own_records

        def swap_cores(x):
            return lax.ppermute(x, "sector", sibling)

        def step_on(x):
            return lax.ppermute(x, "sector", onward)

        def exchange(piece, contract, near):
            begins = near is None
            second = swap_cores(piece)
            order = list(range(4 * half - 4))
            left = []
            if near is None:
                first, second = lax.optimization_barrier((piece, second))
                near = prepare(second)
            else:
                first = piece
                left = [contract(0, piece, near, left)]
                left = [contract(1, second, near, left)]
                order = order[2:]
            pieces = [piece, second]
            for step in range(1, half):
                first = step_on(first)
                if step == 1 and not left:
                    first, counts = lax.optimization_barrier((first, near[2]))
                    near = (*near[:2], counts, *near[3:])
                pieces += [first, swap_cores(first)]
                second = step_on(second)
                pieces += [second, swap_cores(second)]
            first = step_on(first)
            for p in order:
                left = [contract(p, pieces[p], near, left)]
            first, left[0] = lax.optimization_barrier((first, left[0]))
            pieces += [first, swap_cores(first)]
            for p in range(4 * half - 4, 4 * half):
                more = [right_flat, wavefunction] if begins and p == 4 * half - 2 else []
                left = [contract(p, pieces[p], near, left, *more)]
            return pieces, near, left[0]

    else:
        capacity = max(1, 2 * records // peers)
        source = own_records // tile_dev
        local = own_records % tile_dev
        is_self = source == own
        hot = ((source[:, None] == devices[None, :]) & ~is_self[:, None]).astype(jnp.int32)
        rank = jnp.sum(hot * jnp.cumsum(hot, axis=0), axis=1) - 1
        every = lookup.reshape(peers, records)
        wanted = ((every // tile_dev == own) & (devices != own)[:, None]).astype(jnp.int32)
        order = jnp.cumsum(wanted, axis=1) - 1
        slots = jnp.arange(capacity, dtype=jnp.int32)
        chosen = wanted[:, :, None] * (order[:, :, None] == slots).astype(jnp.int32)
        send_index = jnp.sum(chosen * (every % tile_dev)[:, :, None], axis=1).reshape(-1)
        place = jnp.where(is_self, local, tile_dev + source * capacity + rank)
        first_list, second_list = jnp.zeros_like(source), place * tile_rows
        stat_base = (tile_dev + peers * capacity) * tile_rows
        slots = [(0, stat_base + d * STAT_ROWS) for d in range(peers)]

        def exchange(piece, contract, near):
            tiles = piece[:rows].reshape(tile_dev, tile_rows, columns)
            incoming = lax.all_to_all(tiles[send_index], "sector", 0, 0, tiled=True)
            stats = lax.all_gather(piece[rows:], "sector", axis=0, tiled=True)
            buffer = jnp.concatenate([piece[:rows], incoming.reshape(-1, columns), stats], axis=0)
            near = prepare(piece) if near is None else near
            return [buffer], near, contract(0, buffer, near, [])

    vmem = pl.BlockSpec(memory_space=pltpu.VMEM)
    smem = pl.BlockSpec(memory_space=pltpu.SMEM)
    hbm = pl.BlockSpec(memory_space=pltpu.HBM)

    piece = pl.pallas_call(
        start_kernel,
        out_shape=jax.ShapeDtypeStruct((piece_rows, columns), bf16),
        in_specs=[vmem],
        out_specs=vmem,
        compiler_params=pltpu.CompilerParams(vmem_limit_bytes=4 * 2**20),
    )(wavefunction)
    phases = max(p for p, _ in slots) + 1
    env_flat = env_left.reshape(tile_dev * terms * tile_rows, tile_rows)
    right_flat = right_environment_terms.reshape(terms * columns, columns)
    left_type = pltpu.VMEM((shifts * rows, (terms // shifts) * columns), bf16)

    def prepare(marker):
        tied = lax.optimization_barrier((own, first_list, second_list, env_flat, marker))
        counts, lists, places, env_near = pl.pallas_call(
            functools.partial(prepare_kernel, sizes, phases, peers, use_ring),
            out_shape=(
                pltpu.SMEM((phases,), jnp.int32),
                pltpu.SMEM((3, phases * records), jnp.int32),
                pltpu.SMEM((peers,), jnp.int32),
                pltpu.VMEM(env_flat.shape, bf16),
            ),
            in_specs=[smem, hbm, hbm, hbm],
            out_specs=(smem, smem, smem, vmem),
            scratch_shapes=[
                pltpu.SMEM((records,), jnp.int32),
                pltpu.SMEM((records,), jnp.int32),
                pltpu.SemaphoreType.DMA((3,)),
            ],
            compiler_params=pltpu.CompilerParams(vmem_limit_bytes=40 * 2**20),
        )(tied[0].reshape(1), *tied[1:4])
        return env_near, right_flat, counts, lists, places

    def contract(phase, buffer, near, held, *more):
        env_near, right_near, counts, lists, places = near
        return pl.pallas_call(
            functools.partial(left_kernel, phase, 8 if phase == 0 else 10, sizes),
            out_shape=left_type,
            in_specs=[smem, smem] + [vmem] * (2 + len(held) + len(more)),
            out_specs=vmem,
            input_output_aliases={4: 0} if held else {},
            compiler_params=pltpu.CompilerParams(vmem_limit_bytes=4 * 2**20),
            cost_estimate=pl.CostEstimate(
                flops=2**32 if phase == 0 and not held else 2**29,
                bytes_accessed=2**20,
                transcendentals=0,
            ),
        )(counts, lists, buffer, env_near, *held, *more)

    def apply_operator(stage, buffers, near, held, prior, coefs):
        image = pltpu.VMEM((rows, columns), f32)
        small = jax.ShapeDtypeStruct((8, 128), f32)
        send = small if stage == 3 else jax.ShapeDtypeStruct((piece_rows, columns), bf16)
        env_near, right_near, counts, lists, places = near
        operands = [right_near, wavefunction, *buffers, *prior, *coefs, held]
        return pl.pallas_call(
            functools.partial(apply_kernel, stage, sizes, slots),
            out_shape=(image, small, send),
            in_specs=[smem] + [vmem] * len(operands),
            out_specs=(vmem, vmem, vmem),
            scratch_shapes=[pltpu.VMEM((peers * STAT_ROWS, 128), bf16)],
            compiler_params=pltpu.CompilerParams(vmem_limit_bytes=12 * 2**20),
            cost_estimate=pl.CostEstimate(
                flops=4 * rows * terms * tile_rows * columns, bytes_accessed=2**24, transcendentals=0
            ),
        )(places, *operands)

    buffers, near, left = exchange(piece, contract, None)
    image_one, coefs_one, piece = apply_operator(1, buffers, near, left, [], [])
    buffers, near, left = exchange(piece, contract, near)
    image_two, coefs_two, piece = apply_operator(2, buffers, near, left, [image_one], [coefs_one])
    buffers, near, left = exchange(piece, contract, near)
    image_three, coefs_three, stats = apply_operator(
        3, buffers, near, left, [image_one, image_two], [coefs_two]
    )
    distance = 1
    while distance < peers:
        pairs = [(i, i ^ distance) for i in range(peers)]
        stats = stats + lax.ppermute(stats, "sector", pairs)
        distance *= 2
    projected = pl.pallas_call(
        functools.partial(finish_kernel, total),
        out_shape=jax.ShapeDtypeStruct((3, 3), f32),
        in_specs=[vmem, vmem],
        out_specs=vmem,
        compiler_params=pltpu.CompilerParams(vmem_limit_bytes=2 * 2**20),
    )(stats, coefs_three)
    return (image_three, projected)


def solution(mesh):
    return jax.shard_map(
        per_device,
        mesh=mesh,
        in_specs=(
            P(("groups", "sector"), None),
            P(("groups", "sector"), None, None, None),
            P("groups", None, None),
            P("groups", None),
        ),
        out_specs=(P(("groups", "sector"), None), P("groups", None)),
        check_vma=False,
    )
```

```python
import functools

import jax
import jax.numpy as jnp
from jax import lax
from jax.experimental import pallas as pl
from jax.experimental.pallas import tpu as pltpu
from jax.sharding import PartitionSpec as P

epsilon = 1e-06
f32 = jnp.float32
bf16 = jnp.bfloat16
STAT_ROWS = 16
LOADS = 4


def row(value):
    return jnp.broadcast_to(value, (1, 128))


def lane_sums(product):
    return jnp.sum(product, axis=0, keepdims=True)


def split_rows(sums):
    rows = []
    for value in sums:
        high = value.astype(bf16)
        rest = value - high.astype(f32)
        middle = rest.astype(bf16)
        low = (rest - middle.astype(f32)).astype(bf16)
        rows += [high, middle, low]
    rows += [jnp.zeros((1, 128), bf16)] * (STAT_ROWS - len(rows))
    return jnp.concatenate([r.astype(f32) for r in rows], axis=0).astype(bf16)


def start_kernel(w_ref, piece_ref):
    rows = w_ref.shape[0]
    w = w_ref[...]
    piece_ref[0:rows, :] = w
    wide = w.astype(f32)
    piece_ref[rows:, :] = split_rows([lane_sums(wide * wide)])


def ring_place(chip, chips):
    return jnp.where(chip % 2 == 0, chip // 2, chips - 1 - chip // 2)


def prepare_kernel(sizes, phases, peers, ring, own_ref, first_ref, second_ref, env_ref, *rest):
    count_ref, list_ref, stat_ref, env_out, first, second, sems = rest
    tile_dev, shifts, group, tile_rows, total = sizes
    records = tile_dev * shifts
    large = pltpu.make_async_copy(env_ref, env_out, sems.at[0])
    large.start()
    small = [
        pltpu.make_async_copy(first_ref, first, sems.at[1]),
        pltpu.make_async_copy(second_ref, second, sems.at[2]),
    ]
    for copy in small:
        copy.start()
    for p in range(phases):
        count_ref[p] = 0

    if ring:
        own = own_ref[0]
        core = own % 2
        chips = peers // 2
        here = ring_place(own // 2, chips)
        for d in range(peers):
            ahead = here - (d // 4 if d // 2 % 2 == 0 else chips - 1 - d // 4)
            ahead = jnp.where(ahead < 0, ahead + chips, ahead)
            steps = jnp.where(core == 0, ahead, jnp.where(ahead == 0, 0, chips - ahead))
            other = core if d % 2 == 0 else 1 - core
            slot = jnp.where(
                steps < chips // 2, 4 * steps - 2 + 2 * other, 4 * (chips - steps) + 1 - 2 * other
            )
            slot = jnp.where(steps == chips // 2, 2 * chips - 2 + other, slot)
            stat_ref[d] = jnp.where(steps == 0, other, slot) * STAT_ROWS
    else:

        def one_place(d, carry):
            stat_ref[d] = d * STAT_ROWS
            return carry

        lax.fori_loop(0, peers, one_place, 0)
    for copy in small:
        copy.wait()

    def one_tile(tile, carry):
        for shift in range(shifts):
            r = tile * shifts + shift
            if ring:
                source = first[r]
                device = lax.div(source, tile_dev)
                p = lax.div(stat_ref[device], STAT_ROWS)
                offset = (source - device * tile_dev) * tile_rows
            else:
                p, offset = first[r], second[r]
            n = count_ref[p]
            list_ref[0, p * records + n] = offset
            list_ref[1, p * records + n] = r * group * tile_rows
            list_ref[2, p * records + n] = (shift * tile_dev + tile) * tile_rows
            count_ref[p] = n + 1
        return carry

    lax.fori_loop(0, tile_dev, one_tile, 0)
    large.wait()


def contract_left(phase, unroll, sizes, count_ref, list_ref, buf_ref, env_ref, left_ref):
    tile_dev, shifts, group, tile_rows, total = sizes
    base = phase * tile_dev * shifts
    width = group * tile_rows
    count = count_ref[phase]

    def one(n):
        offset = pl.multiple_of(list_ref[0, n], 16)
        start = pl.multiple_of(list_ref[1, n], 128)
        target = pl.multiple_of(list_ref[2, n], 128)
        picked = buf_ref[pl.ds(offset, tile_rows), :]
        for t in range(group):
            left_ref[pl.ds(target, tile_rows), t * 128 : (t + 1) * 128] = jnp.dot(
                env_ref[pl.ds(start + t * tile_rows, tile_rows), :],
                picked,
                preferred_element_type=f32,
            ).astype(bf16)

    def some(j, carry):
        for q in range(unroll):
            one(base + jnp.minimum(j * unroll + q, count - 1))
        return carry

    lax.fori_loop(0, (count + unroll - 1) // unroll, some, 0)


def left_kernel(phase, unroll, sizes, count_ref, list_ref, buf_ref, env_ref, *rest):
    contract_left(phase, unroll, sizes, count_ref, list_ref, buf_ref, env_ref, rest[-1])


def apply_kernel(stage, sizes, slots, stat_ref, right_ref, w_ref, *rest):
    tile_dev, shifts, group, tile_rows, total = sizes
    rows = tile_dev * tile_rows
    phases = max(p for p, _ in slots) + 1
    bufs, rest = rest[:phases], rest[phases:]
    prior, rest = rest[: stage - 1], rest[stage - 1 :]
    if stage > 1:
        coef_in, rest = rest[0], rest[1:]
    left_ref, image_ref, coef_ref, send_ref, all_stats = rest

    width = group * tile_rows
    applied = jnp.zeros((rows, 128), f32)
    for k in range(shifts):
        applied = applied + jnp.dot(
            left_ref[k * rows : (k + 1) * rows, :],
            right_ref[k * width : (k + 1) * width, :],
            preferred_element_type=f32,
        )

    for n, (p, offset) in enumerate(slots):
        all_stats[n * STAT_ROWS : (n + 1) * STAT_ROWS, :] = bufs[p][offset : offset + STAT_ROWS, :]
    gathered = jnp.zeros((STAT_ROWS, 128), f32)
    for d in range(stat_ref.shape[0]):
        offset = pl.multiple_of(stat_ref[d], 16)
        gathered = gathered + all_stats[pl.ds(offset, STAT_ROWS), :].astype(f32)

    def mean_of(j):
        lanes = gathered[3 * j : 3 * j + 1] + gathered[3 * j + 1 : 3 * j + 2]
        lanes = lanes + gathered[3 * j + 2 : 3 * j + 3]
        return row(jnp.sum(lanes, axis=1, keepdims=True) * (1.0 / total))

    w = w_ref[...].astype(f32)
    if stage == 1:
        square = mean_of(0)
        scale = lax.rsqrt(square + epsilon)
        coefs = [scale, scale * scale * square]
        image = scale * applied
        sums = [lane_sums((w * scale) * image), lane_sums(image * image)]
    elif stage == 2:
        scale, g11 = coef_in[0:1, :], coef_in[1:2, :]
        aa, norm = mean_of(0), mean_of(1)
        rest_square = jnp.maximum(norm - 2.0 * aa * aa + aa * aa * g11, 0.0)
        ba = jnp.sqrt(rest_square + epsilon)
        g12 = (aa - aa * g11) / ba
        g22 = rest_square / (ba * ba)
        coefs = [scale, g11, aa, ba, g12, g22]
        first = prior[0][...]
        basis_one = w * scale
        basis_two = (first - aa * basis_one) / ba
        image = (applied - aa * first) / ba
        sums = [
            lane_sums(basis_one * image),
            lane_sums(basis_two * image),
            lane_sums(image * image),
        ]
    else:
        scale, g11, aa, ba, g12, g22 = [coef_in[j : j + 1, :] for j in range(6)]
        ab, bb, norm = mean_of(0), mean_of(1), mean_of(2)
        rest_square = norm - 2.0 * (ab * ab + bb * bb) + ab * ab * g11 + bb * bb * g22
        rest_square = jnp.maximum(rest_square + 2.0 * ab * bb * g12, 0.0)
        cb = jnp.sqrt(rest_square + epsilon)
        coefs = [aa, ab, ba, bb, cb]
        first, second = prior[0][...], prior[1][...]
        basis_one = w * scale
        basis_two = (first - aa * basis_one) / ba
        basis_three = (second - ab * basis_one - bb * basis_two) / cb
        image = (applied - ab * first - bb * second) / cb
        sums = [lane_sums(b * image) for b in (basis_one, basis_two, basis_three)]

    image_ref[...] = image
    coef_ref[...] = jnp.concatenate(coefs + [jnp.zeros((1, 128), f32)] * (8 - len(coefs)), axis=0)
    if stage < 3:
        rows = image.shape[0]
        send_ref[0:rows, :] = image.astype(bf16)
        send_ref[rows:, :] = split_rows(sums)
    else:
        send_ref[...] = jnp.concatenate(sums + [jnp.zeros((1, 128), f32)] * 5, axis=0)


def finish_kernel(total, stat_ref, coef_ref, out_ref):
    last = [row(jnp.sum(stat_ref[j : j + 1, :], axis=1, keepdims=True) * (1.0 / total)) for j in range(3)]
    aa, ab, ba, bb, cb = [coef_ref[j : j + 1, :] for j in range(5)]
    lane = lax.broadcasted_iota(jnp.int32, (1, 128), 1)

    def line(a, b, c):
        return jnp.where(lane == 0, a, jnp.where(lane == 1, b, c))

    zero = jnp.zeros((1, 128), f32)
    table = jnp.concatenate(
        [line(aa, ab, last[0]), line(ba, bb, last[1]), line(zero, cb, last[2])], axis=0
    )
    out_ref[...] = table[:, 0:3]


def ring_pairs(peers):
    chips = peers // 2
    order = list(range(0, chips, 2)) + list(range(chips - 1, 0, -2))
    pairs = []
    for j in range(chips):
        here, after = order[j] * 2, order[(j + 1) % chips] * 2
        pairs += [(here, after), (after + 1, here + 1)]
    return pairs


def per_device(wavefunction, env_left, right_environment_terms, source_tile_lookup):
    peers = lax.axis_size("sector")
    own = lax.axis_index("sector")
    tile_dev, terms, tile_rows = env_left.shape[0], env_left.shape[1], env_left.shape[2]
    rows, columns = wavefunction.shape
    shifts = source_tile_lookup.shape[1]
    records = tile_dev * shifts
    total = peers * rows * columns
    sizes = (tile_dev, shifts, terms // shifts, tile_rows, total)
    piece_rows = rows + STAT_ROWS
    lookup = source_tile_lookup
    own_records = lax.dynamic_slice_in_dim(lookup, own * tile_dev, tile_dev, 0).reshape(records)
    devices = jnp.arange(peers, dtype=jnp.int32)
    use_ring = peers * tile_dev <= 2 * records

    if use_ring:
        chips = peers // 2
        onward = ring_pairs(peers)
        sibling = [(i, i ^ 1) for i in range(peers)]
        half = chips // 2
        slots = [(p, rows) for p in range(peers)]
        first_list = second_list = own_records

        def swap_cores(x):
            return lax.ppermute(x, "sector", sibling)

        def step_on(x):
            return lax.ppermute(x, "sector", onward)

        def exchange(piece, contract, near):
            begins = near is None
            second = swap_cores(piece)
            order = list(range(4 * half - 4))
            left = []
            if near is None:
                first, second = lax.optimization_barrier((piece, second))
                near = prepare(second)
            else:
                first = piece
                left = [contract(0, piece, near, left)]
                left = [contract(1, second, near, left)]
                order = order[2:]
            pieces = [piece, second]
            for step in range(1, half):
                first = step_on(first)
                if step == 1 and not left:
                    first, counts = lax.optimization_barrier((first, near[2]))
                    near = (*near[:2], counts, *near[3:])
                pieces += [first, swap_cores(first)]
                second = step_on(second)
                pieces += [second, swap_cores(second)]
            first = step_on(first)
            for p in order:
                left = [contract(p, pieces[p], near, left)]
            first, left[0] = lax.optimization_barrier((first, left[0]))
            pieces += [first, swap_cores(first)]
            for p in range(4 * half - 4, 4 * half):
                more = [right_flat, wavefunction] if begins and p == 4 * half - 2 else []
                left = [contract(p, pieces[p], near, left, *more)]
            return pieces, near, left[0]

    else:
        capacity = max(1, 2 * records // peers)
        source = own_records // tile_dev
        local = own_records % tile_dev
        is_self = source == own
        hot = ((source[:, None] == devices[None, :]) & ~is_self[:, None]).astype(jnp.int32)
        rank = jnp.sum(hot * jnp.cumsum(hot, axis=0), axis=1) - 1
        every = lookup.reshape(peers, records)
        wanted = ((every // tile_dev == own) & (devices != own)[:, None]).astype(jnp.int32)
        order = jnp.cumsum(wanted, axis=1) - 1
        slots = jnp.arange(capacity, dtype=jnp.int32)
        chosen = wanted[:, :, None] * (order[:, :, None] == slots).astype(jnp.int32)
        send_index = jnp.sum(chosen * (every % tile_dev)[:, :, None], axis=1).reshape(-1)
        place = jnp.where(is_self, local, tile_dev + source * capacity + rank)
        first_list, second_list = jnp.zeros_like(source), place * tile_rows
        stat_base = (tile_dev + peers * capacity) * tile_rows
        slots = [(0, stat_base + d * STAT_ROWS) for d in range(peers)]

        def exchange(piece, contract, near):
            tiles = piece[:rows].reshape(tile_dev, tile_rows, columns)
            incoming = lax.all_to_all(tiles[send_index], "sector", 0, 0, tiled=True)
            stats = lax.all_gather(piece[rows:], "sector", axis=0, tiled=True)
            buffer = jnp.concatenate([piece[:rows], incoming.reshape(-1, columns), stats], axis=0)
            near = prepare(piece) if near is None else near
            return [buffer], near, contract(0, buffer, near, [])

    vmem = pl.BlockSpec(memory_space=pltpu.VMEM)
    smem = pl.BlockSpec(memory_space=pltpu.SMEM)
    hbm = pl.BlockSpec(memory_space=pltpu.HBM)

    piece = pl.pallas_call(
        start_kernel,
        out_shape=jax.ShapeDtypeStruct((piece_rows, columns), bf16),
        in_specs=[vmem],
        out_specs=vmem,
        compiler_params=pltpu.CompilerParams(vmem_limit_bytes=4 * 2**20),
    )(wavefunction)
    phases = max(p for p, _ in slots) + 1
    env_flat = env_left.reshape(tile_dev * terms * tile_rows, tile_rows)
    right_flat = right_environment_terms.reshape(terms * columns, columns)
    left_type = pltpu.VMEM((shifts * rows, (terms // shifts) * columns), bf16)

    def prepare(marker):
        tied = lax.optimization_barrier((own, first_list, second_list, env_flat, marker))
        counts, lists, places, env_near = pl.pallas_call(
            functools.partial(prepare_kernel, sizes, phases, peers, use_ring),
            out_shape=(
                pltpu.SMEM((phases,), jnp.int32),
                pltpu.SMEM((3, phases * records), jnp.int32),
                pltpu.SMEM((peers,), jnp.int32),
                pltpu.VMEM(env_flat.shape, bf16),
            ),
            in_specs=[smem, hbm, hbm, hbm],
            out_specs=(smem, smem, smem, vmem),
            scratch_shapes=[
                pltpu.SMEM((records,), jnp.int32),
                pltpu.SMEM((records,), jnp.int32),
                pltpu.SemaphoreType.DMA((3,)),
            ],
            compiler_params=pltpu.CompilerParams(vmem_limit_bytes=40 * 2**20),
        )(tied[0].reshape(1), *tied[1:4])
        return env_near, right_flat, counts, lists, places

    def contract(phase, buffer, near, held, *more):
        env_near, right_near, counts, lists, places = near
        return pl.pallas_call(
            functools.partial(left_kernel, phase, 10 if phase > peers - 3 else 5, sizes),
            out_shape=left_type,
            in_specs=[smem, smem] + [vmem] * (2 + len(held) + len(more)),
            out_specs=vmem,
            input_output_aliases={4: 0} if held else {},
            compiler_params=pltpu.CompilerParams(vmem_limit_bytes=4 * 2**20),
            cost_estimate=pl.CostEstimate(
                flops=2**32 if phase == 0 and not held else 2**29,
                bytes_accessed=2**20,
                transcendentals=0,
            ),
        )(counts, lists, buffer, env_near, *held, *more)

    def apply_operator(stage, buffers, near, held, prior, coefs):
        image = pltpu.VMEM((rows, columns), f32)
        small = jax.ShapeDtypeStruct((8, 128), f32)
        send = small if stage == 3 else jax.ShapeDtypeStruct((piece_rows, columns), bf16)
        env_near, right_near, counts, lists, places = near
        operands = [right_near, wavefunction, *buffers, *prior, *coefs, held]
        return pl.pallas_call(
            functools.partial(apply_kernel, stage, sizes, slots),
            out_shape=(image, small, send),
            in_specs=[smem] + [vmem] * len(operands),
            out_specs=(vmem, vmem, vmem),
            scratch_shapes=[pltpu.VMEM((peers * STAT_ROWS, 128), bf16)],
            compiler_params=pltpu.CompilerParams(vmem_limit_bytes=12 * 2**20),
            cost_estimate=pl.CostEstimate(
                flops=4 * rows * terms * tile_rows * columns, bytes_accessed=2**24, transcendentals=0
            ),
        )(places, *operands)

    buffers, near, left = exchange(piece, contract, None)
    image_one, coefs_one, piece = apply_operator(1, buffers, near, left, [], [])
    buffers, near, left = exchange(piece, contract, near)
    image_two, coefs_two, piece = apply_operator(2, buffers, near, left, [image_one], [coefs_one])
    buffers, near, left = exchange(piece, contract, near)
    image_three, coefs_three, stats = apply_operator(
        3, buffers, near, left, [image_one, image_two], [coefs_two]
    )
    distance = 1
    while distance < peers:
        pairs = [(i, i ^ distance) for i in range(peers)]
        stats = stats + lax.ppermute(stats, "sector", pairs)
        distance *= 2
    projected = pl.pallas_call(
        functools.partial(finish_kernel, total),
        out_shape=jax.ShapeDtypeStruct((3, 3), f32),
        in_specs=[vmem, vmem],
        out_specs=vmem,
        compiler_params=pltpu.CompilerParams(vmem_limit_bytes=2 * 2**20),
    )(stats, coefs_three)
    return (image_three, projected)


def solution(mesh):
    return jax.shard_map(
        per_device,
        mesh=mesh,
        in_specs=(
            P(("groups", "sector"), None),
            P(("groups", "sector"), None, None, None),
            P("groups", None, None),
            P("groups", None),
        ),
        out_specs=(P(("groups", "sector"), None), P("groups", None)),
        check_vma=False,
    )
```

```python
import functools

import jax
import jax.numpy as jnp
from jax import lax
from jax.experimental import pallas as pl
from jax.experimental.pallas import tpu as pltpu
from jax.sharding import PartitionSpec as P

epsilon = 1e-06
f32 = jnp.float32
bf16 = jnp.bfloat16
STAT_ROWS = 16
LOADS = 4


def row(value):
    return jnp.broadcast_to(value, (1, 128))


def lane_sums(product):
    return jnp.sum(product, axis=0, keepdims=True)


def split_rows(sums):
    rows = []
    for value in sums:
        high = value.astype(bf16)
        rest = value - high.astype(f32)
        middle = rest.astype(bf16)
        low = (rest - middle.astype(f32)).astype(bf16)
        rows += [high, middle, low]
    rows += [jnp.zeros((1, 128), bf16)] * (STAT_ROWS - len(rows))
    return jnp.concatenate([r.astype(f32) for r in rows], axis=0).astype(bf16)


def start_kernel(w_ref, piece_ref):
    rows = w_ref.shape[0]
    w = w_ref[...]
    piece_ref[0:rows, :] = w
    wide = w.astype(f32)
    piece_ref[rows:, :] = split_rows([lane_sums(wide * wide)])


def ring_place(chip, chips):
    return jnp.where(chip % 2 == 0, chip // 2, chips - 1 - chip // 2)


def prepare_kernel(sizes, phases, peers, ring, own_ref, first_ref, second_ref, env_ref, *rest):
    count_ref, list_ref, stat_ref, env_out, first, second, sems = rest
    tile_dev, shifts, group, tile_rows, total = sizes
    records = tile_dev * shifts
    large = pltpu.make_async_copy(env_ref, env_out, sems.at[0])
    large.start()
    small = [
        pltpu.make_async_copy(first_ref, first, sems.at[1]),
        pltpu.make_async_copy(second_ref, second, sems.at[2]),
    ]
    for copy in small:
        copy.start()
    for p in range(phases):
        count_ref[p] = 0

    if ring:
        own = own_ref[0]
        core = own % 2
        chips = peers // 2
        here = ring_place(own // 2, chips)
        for d in range(peers):
            ahead = here - (d // 4 if d // 2 % 2 == 0 else chips - 1 - d // 4)
            ahead = jnp.where(ahead < 0, ahead + chips, ahead)
            steps = jnp.where(core == 0, ahead, jnp.where(ahead == 0, 0, chips - ahead))
            other = core if d % 2 == 0 else 1 - core
            slot = jnp.where(
                steps < chips // 2, 4 * steps - 2 + 2 * other, 4 * (chips - steps) + 1 - 2 * other
            )
            slot = jnp.where(steps == chips // 2, 2 * chips - 2 + other, slot)
            stat_ref[d] = jnp.where(steps == 0, other, slot) * STAT_ROWS
    else:

        def one_place(d, carry):
            stat_ref[d] = d * STAT_ROWS
            return carry

        lax.fori_loop(0, peers, one_place, 0)
    for copy in small:
        copy.wait()

    def one_tile(tile, carry):
        for shift in range(shifts):
            r = tile * shifts + shift
            if ring:
                source = first[r]
                device = lax.div(source, tile_dev)
                p = lax.div(stat_ref[device], STAT_ROWS)
                offset = (source - device * tile_dev) * tile_rows
            else:
                p, offset = first[r], second[r]
            n = count_ref[p]
            list_ref[0, p * records + n] = offset
            list_ref[1, p * records + n] = r * group * tile_rows
            list_ref[2, p * records + n] = (shift * tile_dev + tile) * tile_rows
            count_ref[p] = n + 1
        return carry

    lax.fori_loop(0, tile_dev, one_tile, 0)
    large.wait()


def contract_left(phase, unroll, sizes, count_ref, list_ref, buf_ref, env_ref, left_ref):
    tile_dev, shifts, group, tile_rows, total = sizes
    base = phase * tile_dev * shifts
    width = group * tile_rows
    count = count_ref[phase]

    def one(n):
        offset = pl.multiple_of(list_ref[0, n], 16)
        start = pl.multiple_of(list_ref[1, n], 128)
        target = pl.multiple_of(list_ref[2, n], 128)
        picked = buf_ref[pl.ds(offset, tile_rows), :]
        for t in range(group):
            left_ref[pl.ds(target, tile_rows), t * 128 : (t + 1) * 128] = jnp.dot(
                env_ref[pl.ds(start + t * tile_rows, tile_rows), :],
                picked,
                preferred_element_type=f32,
            ).astype(bf16)

    def some(j, carry):
        for q in range(unroll):
            one(base + jnp.minimum(j * unroll + q, count - 1))
        return carry

    lax.fori_loop(0, (count + unroll - 1) // unroll, some, 0)


def left_kernel(phase, unroll, sizes, count_ref, list_ref, buf_ref, env_ref, *rest):
    contract_left(phase, unroll, sizes, count_ref, list_ref, buf_ref, env_ref, rest[-1])


def apply_kernel(stage, sizes, slots, stat_ref, right_ref, w_ref, *rest):
    tile_dev, shifts, group, tile_rows, total = sizes
    rows = tile_dev * tile_rows
    phases = max(p for p, _ in slots) + 1
    bufs, rest = rest[:phases], rest[phases:]
    prior, rest = rest[: stage - 1], rest[stage - 1 :]
    if stage > 1:
        coef_in, rest = rest[0], rest[1:]
    left_ref, image_ref, coef_ref, send_ref, all_stats = rest

    width = group * tile_rows
    applied = jnp.zeros((rows, 128), f32)
    for k in range(shifts):
        applied = applied + jnp.dot(
            left_ref[k * rows : (k + 1) * rows, :],
            right_ref[k * width : (k + 1) * width, :],
            preferred_element_type=f32,
        )

    for n, (p, offset) in enumerate(slots):
        all_stats[n * STAT_ROWS : (n + 1) * STAT_ROWS, :] = bufs[p][offset : offset + STAT_ROWS, :]
    gathered = jnp.zeros((STAT_ROWS, 128), f32)
    for d in range(stat_ref.shape[0]):
        offset = pl.multiple_of(stat_ref[d], 16)
        gathered = gathered + all_stats[pl.ds(offset, STAT_ROWS), :].astype(f32)

    def mean_of(j):
        lanes = gathered[3 * j : 3 * j + 1] + gathered[3 * j + 1 : 3 * j + 2]
        lanes = lanes + gathered[3 * j + 2 : 3 * j + 3]
        return row(jnp.sum(lanes, axis=1, keepdims=True) * (1.0 / total))

    w = w_ref[...].astype(f32)
    if stage == 1:
        square = mean_of(0)
        scale = lax.rsqrt(square + epsilon)
        coefs = [scale, scale * scale * square]
        image = scale * applied
        sums = [lane_sums((w * scale) * image), lane_sums(image * image)]
    elif stage == 2:
        scale, g11 = coef_in[0:1, :], coef_in[1:2, :]
        aa, norm = mean_of(0), mean_of(1)
        rest_square = jnp.maximum(norm - 2.0 * aa * aa + aa * aa * g11, 0.0)
        ba = jnp.sqrt(rest_square + epsilon)
        g12 = (aa - aa * g11) / ba
        g22 = rest_square / (ba * ba)
        coefs = [scale, g11, aa, ba, g12, g22]
        first = prior[0][...]
        basis_one = w * scale
        basis_two = (first - aa * basis_one) / ba
        image = (applied - aa * first) / ba
        sums = [
            lane_sums(basis_one * image),
            lane_sums(basis_two * image),
            lane_sums(image * image),
        ]
    else:
        scale, g11, aa, ba, g12, g22 = [coef_in[j : j + 1, :] for j in range(6)]
        ab, bb, norm = mean_of(0), mean_of(1), mean_of(2)
        rest_square = norm - 2.0 * (ab * ab + bb * bb) + ab * ab * g11 + bb * bb * g22
        rest_square = jnp.maximum(rest_square + 2.0 * ab * bb * g12, 0.0)
        cb = jnp.sqrt(rest_square + epsilon)
        coefs = [aa, ab, ba, bb, cb]
        first, second = prior[0][...], prior[1][...]
        basis_one = w * scale
        basis_two = (first - aa * basis_one) / ba
        basis_three = (second - ab * basis_one - bb * basis_two) / cb
        image = (applied - ab * first - bb * second) / cb
        sums = [lane_sums(b * image) for b in (basis_one, basis_two, basis_three)]

    image_ref[...] = image
    coef_ref[...] = jnp.concatenate(coefs + [jnp.zeros((1, 128), f32)] * (8 - len(coefs)), axis=0)
    if stage < 3:
        rows = image.shape[0]
        send_ref[0:rows, :] = image.astype(bf16)
        send_ref[rows:, :] = split_rows(sums)
    else:
        send_ref[...] = jnp.concatenate(sums + [jnp.zeros((1, 128), f32)] * 5, axis=0)


def finish_kernel(total, stat_ref, coef_ref, out_ref):
    last = [row(jnp.sum(stat_ref[j : j + 1, :], axis=1, keepdims=True) * (1.0 / total)) for j in range(3)]
    aa, ab, ba, bb, cb = [coef_ref[j : j + 1, :] for j in range(5)]
    lane = lax.broadcasted_iota(jnp.int32, (1, 128), 1)

    def line(a, b, c):
        return jnp.where(lane == 0, a, jnp.where(lane == 1, b, c))

    zero = jnp.zeros((1, 128), f32)
    table = jnp.concatenate(
        [line(aa, ab, last[0]), line(ba, bb, last[1]), line(zero, cb, last[2])], axis=0
    )
    out_ref[...] = table[:, 0:3]


def ring_pairs(peers):
    chips = peers // 2
    order = list(range(0, chips, 2)) + list(range(chips - 1, 0, -2))
    pairs = []
    for j in range(chips):
        here, after = order[j] * 2, order[(j + 1) % chips] * 2
        pairs += [(here, after), (after + 1, here + 1)]
    return pairs


def per_device(wavefunction, env_left, right_environment_terms, source_tile_lookup):
    peers = lax.axis_size("sector")
    own = lax.axis_index("sector")
    tile_dev, terms, tile_rows = env_left.shape[0], env_left.shape[1], env_left.shape[2]
    rows, columns = wavefunction.shape
    shifts = source_tile_lookup.shape[1]
    records = tile_dev * shifts
    total = peers * rows * columns
    sizes = (tile_dev, shifts, terms // shifts, tile_rows, total)
    piece_rows = rows + STAT_ROWS
    lookup = source_tile_lookup
    own_records = lax.dynamic_slice_in_dim(lookup, own * tile_dev, tile_dev, 0).reshape(records)
    devices = jnp.arange(peers, dtype=jnp.int32)
    use_ring = peers * tile_dev <= 2 * records

    if use_ring:
        chips = peers // 2
        onward = ring_pairs(peers)
        sibling = [(i, i ^ 1) for i in range(peers)]
        half = chips // 2
        slots = [(p, rows) for p in range(peers)]
        first_list = second_list = own_records

        def swap_cores(x):
            return lax.ppermute(x, "sector", sibling)

        def step_on(x):
            return lax.ppermute(x, "sector", onward)

        def exchange(piece, contract, near):
            begins = near is None
            second = swap_cores(piece)
            order = list(range(4 * half - 4))
            left = []
            if near is None:
                first, second = lax.optimization_barrier((piece, second))
                near = prepare(second)
            else:
                first = piece
                left = [contract(0, piece, near, left)]
                left = [contract(1, second, near, left)]
                order = order[2:]
            pieces = [piece, second]
            for step in range(1, half):
                first = step_on(first)
                if step == 1 and not left:
                    first, counts = lax.optimization_barrier((first, near[2]))
                    near = (*near[:2], counts, *near[3:])
                pieces += [first, swap_cores(first)]
                second = step_on(second)
                pieces += [second, swap_cores(second)]
            first = step_on(first)
            for p in order:
                left = [contract(p, pieces[p], near, left)]
            first, left[0] = lax.optimization_barrier((first, left[0]))
            pieces += [first, swap_cores(first)]
            for p in range(4 * half - 4, 4 * half):
                more = [right_flat, wavefunction] if begins and p == 4 * half - 2 else []
                left = [contract(p, pieces[p], near, left, *more)]
            return pieces, near, left[0]

    else:
        capacity = max(1, 2 * records // peers)
        source = own_records // tile_dev
        local = own_records % tile_dev
        is_self = source == own
        hot = ((source[:, None] == devices[None, :]) & ~is_self[:, None]).astype(jnp.int32)
        rank = jnp.sum(hot * jnp.cumsum(hot, axis=0), axis=1) - 1
        every = lookup.reshape(peers, records)
        wanted = ((every // tile_dev == own) & (devices != own)[:, None]).astype(jnp.int32)
        order = jnp.cumsum(wanted, axis=1) - 1
        slots = jnp.arange(capacity, dtype=jnp.int32)
        chosen = wanted[:, :, None] * (order[:, :, None] == slots).astype(jnp.int32)
        send_index = jnp.sum(chosen * (every % tile_dev)[:, :, None], axis=1).reshape(-1)
        place = jnp.where(is_self, local, tile_dev + source * capacity + rank)
        first_list, second_list = jnp.zeros_like(source), place * tile_rows
        stat_base = (tile_dev + peers * capacity) * tile_rows
        slots = [(0, stat_base + d * STAT_ROWS) for d in range(peers)]

        def exchange(piece, contract, near):
            tiles = piece[:rows].reshape(tile_dev, tile_rows, columns)
            incoming = lax.all_to_all(tiles[send_index], "sector", 0, 0, tiled=True)
            stats = lax.all_gather(piece[rows:], "sector", axis=0, tiled=True)
            buffer = jnp.concatenate([piece[:rows], incoming.reshape(-1, columns), stats], axis=0)
            near = prepare(piece) if near is None else near
            return [buffer], near, contract(0, buffer, near, [])

    vmem = pl.BlockSpec(memory_space=pltpu.VMEM)
    smem = pl.BlockSpec(memory_space=pltpu.SMEM)
    hbm = pl.BlockSpec(memory_space=pltpu.HBM)

    piece = pl.pallas_call(
        start_kernel,
        out_shape=jax.ShapeDtypeStruct((piece_rows, columns), bf16),
        in_specs=[vmem],
        out_specs=vmem,
        compiler_params=pltpu.CompilerParams(vmem_limit_bytes=4 * 2**20),
    )(wavefunction)
    phases = max(p for p, _ in slots) + 1
    env_flat = env_left.reshape(tile_dev * terms * tile_rows, tile_rows)
    right_flat = right_environment_terms.reshape(terms * columns, columns)
    left_type = pltpu.VMEM((shifts * rows, (terms // shifts) * columns), bf16)

    def prepare(marker):
        tied = lax.optimization_barrier((own, first_list, second_list, env_flat, marker))
        counts, lists, places, env_near = pl.pallas_call(
            functools.partial(prepare_kernel, sizes, phases, peers, use_ring),
            out_shape=(
                pltpu.SMEM((phases,), jnp.int32),
                pltpu.SMEM((3, phases * records), jnp.int32),
                pltpu.SMEM((peers,), jnp.int32),
                pltpu.VMEM(env_flat.shape, bf16),
            ),
            in_specs=[smem, hbm, hbm, hbm],
            out_specs=(smem, smem, smem, vmem),
            scratch_shapes=[
                pltpu.SMEM((records,), jnp.int32),
                pltpu.SMEM((records,), jnp.int32),
                pltpu.SemaphoreType.DMA((3,)),
            ],
            compiler_params=pltpu.CompilerParams(vmem_limit_bytes=40 * 2**20),
        )(tied[0].reshape(1), *tied[1:4])
        return env_near, right_flat, counts, lists, places

    def contract(phase, buffer, near, held, *more):
        env_near, right_near, counts, lists, places = near
        return pl.pallas_call(
            functools.partial(left_kernel, phase, 10 if phase > peers - 5 else 4, sizes),
            out_shape=left_type,
            in_specs=[smem, smem] + [vmem] * (2 + len(held) + len(more)),
            out_specs=vmem,
            input_output_aliases={4: 0} if held else {},
            compiler_params=pltpu.CompilerParams(vmem_limit_bytes=4 * 2**20),
            cost_estimate=pl.CostEstimate(
                flops=2**32 if phase == 0 and not held else 2**29,
                bytes_accessed=2**20,
                transcendentals=0,
            ),
        )(counts, lists, buffer, env_near, *held, *more)

    def apply_operator(stage, buffers, near, held, prior, coefs):
        image = pltpu.VMEM((rows, columns), f32)
        small = jax.ShapeDtypeStruct((8, 128), f32)
        send = small if stage == 3 else jax.ShapeDtypeStruct((piece_rows, columns), bf16)
        env_near, right_near, counts, lists, places = near
        operands = [right_near, wavefunction, *buffers, *prior, *coefs, held]
        return pl.pallas_call(
            functools.partial(apply_kernel, stage, sizes, slots),
            out_shape=(image, small, send),
            in_specs=[smem] + [vmem] * len(operands),
            out_specs=(vmem, vmem, vmem),
            scratch_shapes=[pltpu.VMEM((peers * STAT_ROWS, 128), bf16)],
            compiler_params=pltpu.CompilerParams(vmem_limit_bytes=12 * 2**20),
            cost_estimate=pl.CostEstimate(
                flops=4 * rows * terms * tile_rows * columns, bytes_accessed=2**24, transcendentals=0
            ),
        )(places, *operands)

    buffers, near, left = exchange(piece, contract, None)
    image_one, coefs_one, piece = apply_operator(1, buffers, near, left, [], [])
    buffers, near, left = exchange(piece, contract, near)
    image_two, coefs_two, piece = apply_operator(2, buffers, near, left, [image_one], [coefs_one])
    buffers, near, left = exchange(piece, contract, near)
    image_three, coefs_three, stats = apply_operator(
        3, buffers, near, left, [image_one, image_two], [coefs_two]
    )
    distance = 1
    while distance < peers:
        pairs = [(i, i ^ distance) for i in range(peers)]
        stats = stats + lax.ppermute(stats, "sector", pairs)
        distance *= 2
    projected = pl.pallas_call(
        functools.partial(finish_kernel, total),
        out_shape=jax.ShapeDtypeStruct((3, 3), f32),
        in_specs=[vmem, vmem],
        out_specs=vmem,
        compiler_params=pltpu.CompilerParams(vmem_limit_bytes=2 * 2**20),
    )(stats, coefs_three)
    return (image_three, projected)


def solution(mesh):
    return jax.shard_map(
        per_device,
        mesh=mesh,
        in_specs=(
            P(("groups", "sector"), None),
            P(("groups", "sector"), None, None, None),
            P("groups", None, None),
            P("groups", None),
        ),
        out_specs=(P(("groups", "sector"), None), P("groups", None)),
        check_vma=False,
    )
```

```python
import functools

import jax
import jax.numpy as jnp
from jax import lax
from jax.experimental import pallas as pl
from jax.experimental.pallas import tpu as pltpu
from jax.sharding import PartitionSpec as P

epsilon = 1e-06
f32 = jnp.float32
bf16 = jnp.bfloat16
STAT_ROWS = 16
LOADS = 4


def row(value):
    return jnp.broadcast_to(value, (1, 128))


def lane_sums(product):
    return jnp.sum(product, axis=0, keepdims=True)


def split_rows(sums):
    rows = []
    for value in sums:
        high = value.astype(bf16)
        rest = value - high.astype(f32)
        middle = rest.astype(bf16)
        low = (rest - middle.astype(f32)).astype(bf16)
        rows += [high, middle, low]
    rows += [jnp.zeros((1, 128), bf16)] * (STAT_ROWS - len(rows))
    return jnp.concatenate([r.astype(f32) for r in rows], axis=0).astype(bf16)


def start_kernel(w_ref, piece_ref):
    rows = w_ref.shape[0]
    w = w_ref[...]
    piece_ref[0:rows, :] = w
    wide = w.astype(f32)
    piece_ref[rows:, :] = split_rows([lane_sums(wide * wide)])


def ring_place(chip, chips):
    return jnp.where(chip % 2 == 0, chip // 2, chips - 1 - chip // 2)


def prepare_kernel(sizes, phases, peers, ring, own_ref, first_ref, second_ref, env_ref, *rest):
    count_ref, list_ref, stat_ref, env_out, first, second, sems = rest
    tile_dev, shifts, group, tile_rows, total = sizes
    records = tile_dev * shifts
    large = pltpu.make_async_copy(env_ref, env_out, sems.at[0])
    large.start()
    small = [
        pltpu.make_async_copy(first_ref, first, sems.at[1]),
        pltpu.make_async_copy(second_ref, second, sems.at[2]),
    ]
    for copy in small:
        copy.start()
    for p in range(phases):
        count_ref[p] = 0

    if ring:
        own = own_ref[0]
        core = own % 2
        chips = peers // 2
        here = ring_place(own // 2, chips)
        for d in range(peers):
            ahead = here - (d // 4 if d // 2 % 2 == 0 else chips - 1 - d // 4)
            ahead = jnp.where(ahead < 0, ahead + chips, ahead)
            steps = jnp.where(core == 0, ahead, jnp.where(ahead == 0, 0, chips - ahead))
            other = core if d % 2 == 0 else 1 - core
            slot = jnp.where(
                steps < chips // 2, 4 * steps - 2 + 2 * other, 4 * (chips - steps) + 1 - 2 * other
            )
            slot = jnp.where(steps == chips // 2, 2 * chips - 2 + other, slot)
            stat_ref[d] = jnp.where(steps == 0, other, slot) * STAT_ROWS
    else:

        def one_place(d, carry):
            stat_ref[d] = d * STAT_ROWS
            return carry

        lax.fori_loop(0, peers, one_place, 0)
    for copy in small:
        copy.wait()

    def one_tile(tile, carry):
        for shift in range(shifts):
            r = tile * shifts + shift
            if ring:
                source = first[r]
                device = lax.div(source, tile_dev)
                p = lax.div(stat_ref[device], STAT_ROWS)
                offset = (source - device * tile_dev) * tile_rows
            else:
                p, offset = first[r], second[r]
            n = count_ref[p]
            list_ref[0, p * records + n] = offset
            list_ref[1, p * records + n] = r * group * tile_rows
            list_ref[2, p * records + n] = (shift * tile_dev + tile) * tile_rows
            count_ref[p] = n + 1
        return carry

    lax.fori_loop(0, tile_dev, one_tile, 0)
    large.wait()


def contract_left(phase, unroll, sizes, count_ref, list_ref, buf_ref, env_ref, left_ref):
    tile_dev, shifts, group, tile_rows, total = sizes
    base = phase * tile_dev * shifts
    width = group * tile_rows
    count = count_ref[phase]

    def one(n):
        offset = pl.multiple_of(list_ref[0, n], 16)
        start = pl.multiple_of(list_ref[1, n], 128)
        target = pl.multiple_of(list_ref[2, n], 128)
        picked = buf_ref[pl.ds(offset, tile_rows), :]
        for t in range(group):
            left_ref[pl.ds(target, tile_rows), t * 128 : (t + 1) * 128] = jnp.dot(
                env_ref[pl.ds(start + t * tile_rows, tile_rows), :],
                picked,
                preferred_element_type=f32,
            ).astype(bf16)

    def some(j, carry):
        for q in range(unroll):
            one(base + jnp.minimum(j * unroll + q, count - 1))
        return carry

    lax.fori_loop(0, (count + unroll - 1) // unroll, some, 0)


def left_kernel(phase, unroll, sizes, count_ref, list_ref, buf_ref, env_ref, *rest):
    contract_left(phase, unroll, sizes, count_ref, list_ref, buf_ref, env_ref, rest[-1])


def apply_kernel(stage, sizes, slots, stat_ref, right_ref, w_ref, *rest):
    tile_dev, shifts, group, tile_rows, total = sizes
    rows = tile_dev * tile_rows
    phases = max(p for p, _ in slots) + 1
    bufs, rest = rest[:phases], rest[phases:]
    prior, rest = rest[: stage - 1], rest[stage - 1 :]
    if stage > 1:
        coef_in, rest = rest[0], rest[1:]
    left_ref, image_ref, coef_ref, send_ref, all_stats = rest

    width = group * tile_rows
    applied = jnp.zeros((rows, 128), f32)
    for k in range(shifts):
        applied = applied + jnp.dot(
            left_ref[k * rows : (k + 1) * rows, :],
            right_ref[k * width : (k + 1) * width, :],
            preferred_element_type=f32,
        )

    for n, (p, offset) in enumerate(slots):
        all_stats[n * STAT_ROWS : (n + 1) * STAT_ROWS, :] = bufs[p][offset : offset + STAT_ROWS, :]
    gathered = jnp.zeros((STAT_ROWS, 128), f32)
    for d in range(stat_ref.shape[0]):
        offset = pl.multiple_of(stat_ref[d], 16)
        gathered = gathered + all_stats[pl.ds(offset, STAT_ROWS), :].astype(f32)

    def mean_of(j):
        lanes = gathered[3 * j : 3 * j + 1] + gathered[3 * j + 1 : 3 * j + 2]
        lanes = lanes + gathered[3 * j + 2 : 3 * j + 3]
        return row(jnp.sum(lanes, axis=1, keepdims=True) * (1.0 / total))

    w = w_ref[...].astype(f32)
    if stage == 1:
        square = mean_of(0)
        scale = lax.rsqrt(square + epsilon)
        coefs = [scale, scale * scale * square]
        image = scale * applied
        sums = [lane_sums((w * scale) * image), lane_sums(image * image)]
    elif stage == 2:
        scale, g11 = coef_in[0:1, :], coef_in[1:2, :]
        aa, norm = mean_of(0), mean_of(1)
        rest_square = jnp.maximum(norm - 2.0 * aa * aa + aa * aa * g11, 0.0)
        ba = jnp.sqrt(rest_square + epsilon)
        g12 = (aa - aa * g11) / ba
        g22 = rest_square / (ba * ba)
        coefs = [scale, g11, aa, ba, g12, g22]
        first = prior[0][...]
        basis_one = w * scale
        basis_two = (first - aa * basis_one) / ba
        image = (applied - aa * first) / ba
        sums = [
            lane_sums(basis_one * image),
            lane_sums(basis_two * image),
            lane_sums(image * image),
        ]
    else:
        scale, g11, aa, ba, g12, g22 = [coef_in[j : j + 1, :] for j in range(6)]
        ab, bb, norm = mean_of(0), mean_of(1), mean_of(2)
        rest_square = norm - 2.0 * (ab * ab + bb * bb) + ab * ab * g11 + bb * bb * g22
        rest_square = jnp.maximum(rest_square + 2.0 * ab * bb * g12, 0.0)
        cb = jnp.sqrt(rest_square + epsilon)
        coefs = [aa, ab, ba, bb, cb]
        first, second = prior[0][...], prior[1][...]
        basis_one = w * scale
        basis_two = (first - aa * basis_one) / ba
        basis_three = (second - ab * basis_one - bb * basis_two) / cb
        image = (applied - ab * first - bb * second) / cb
        sums = [lane_sums(b * image) for b in (basis_one, basis_two, basis_three)]

    image_ref[...] = image
    coef_ref[...] = jnp.concatenate(coefs + [jnp.zeros((1, 128), f32)] * (8 - len(coefs)), axis=0)
    if stage < 3:
        rows = image.shape[0]
        send_ref[0:rows, :] = image.astype(bf16)
        send_ref[rows:, :] = split_rows(sums)
    else:
        send_ref[...] = jnp.concatenate(sums + [jnp.zeros((1, 128), f32)] * 5, axis=0)


def finish_kernel(total, stat_ref, coef_ref, out_ref):
    last = [row(jnp.sum(stat_ref[j : j + 1, :], axis=1, keepdims=True) * (1.0 / total)) for j in range(3)]
    aa, ab, ba, bb, cb = [coef_ref[j : j + 1, :] for j in range(5)]
    lane = lax.broadcasted_iota(jnp.int32, (1, 128), 1)

    def line(a, b, c):
        return jnp.where(lane == 0, a, jnp.where(lane == 1, b, c))

    zero = jnp.zeros((1, 128), f32)
    table = jnp.concatenate(
        [line(aa, ab, last[0]), line(ba, bb, last[1]), line(zero, cb, last[2])], axis=0
    )
    out_ref[...] = table[:, 0:3]


def ring_pairs(peers):
    chips = peers // 2
    order = list(range(0, chips, 2)) + list(range(chips - 1, 0, -2))
    pairs = []
    for j in range(chips):
        here, after = order[j] * 2, order[(j + 1) % chips] * 2
        pairs += [(here, after), (after + 1, here + 1)]
    return pairs


def per_device(wavefunction, env_left, right_environment_terms, source_tile_lookup):
    peers = lax.axis_size("sector")
    own = lax.axis_index("sector")
    tile_dev, terms, tile_rows = env_left.shape[0], env_left.shape[1], env_left.shape[2]
    rows, columns = wavefunction.shape
    shifts = source_tile_lookup.shape[1]
    records = tile_dev * shifts
    total = peers * rows * columns
    sizes = (tile_dev, shifts, terms // shifts, tile_rows, total)
    piece_rows = rows + STAT_ROWS
    lookup = source_tile_lookup
    own_records = lax.dynamic_slice_in_dim(lookup, own * tile_dev, tile_dev, 0).reshape(records)
    devices = jnp.arange(peers, dtype=jnp.int32)
    use_ring = peers * tile_dev <= 2 * records

    if use_ring:
        chips = peers // 2
        onward = ring_pairs(peers)
        sibling = [(i, i ^ 1) for i in range(peers)]
        half = chips // 2
        slots = [(p, rows) for p in range(peers)]
        first_list = second_list = own_records

        def swap_cores(x):
            return lax.ppermute(x, "sector", sibling)

        def step_on(x):
            return lax.ppermute(x, "sector", onward)

        def exchange(piece, contract, near):
            begins = near is None
            second = swap_cores(piece)
            order = list(range(4 * half - 4))
            left = []
            if near is None:
                first, second = lax.optimization_barrier((piece, second))
                near = prepare(second)
            else:
                first = piece
                left = [contract(0, piece, near, left)]
                left = [contract(1, second, near, left)]
                order = order[2:]
            pieces = [piece, second]
            for step in range(1, half):
                first = step_on(first)
                if step == 1 and not left:
                    first, counts = lax.optimization_barrier((first, near[2]))
                    near = (*near[:2], counts, *near[3:])
                pieces += [first, swap_cores(first)]
                second = step_on(second)
                pieces += [second, swap_cores(second)]
            first = step_on(first)
            for p in order:
                left = [contract(p, pieces[p], near, left)]
            first, left[0] = lax.optimization_barrier((first, left[0]))
            pieces += [first, swap_cores(first)]
            for p in range(4 * half - 4, 4 * half):
                more = [right_flat, wavefunction] if begins and p == 4 * half - 2 else []
                left = [contract(p, pieces[p], near, left, *more)]
            return pieces, near, left[0]

    else:
        capacity = max(1, 2 * records // peers)
        source = own_records // tile_dev
        local = own_records % tile_dev
        is_self = source == own
        hot = ((source[:, None] == devices[None, :]) & ~is_self[:, None]).astype(jnp.int32)
        rank = jnp.sum(hot * jnp.cumsum(hot, axis=0), axis=1) - 1
        every = lookup.reshape(peers, records)
        wanted = ((every // tile_dev == own) & (devices != own)[:, None]).astype(jnp.int32)
        order = jnp.cumsum(wanted, axis=1) - 1
        slots = jnp.arange(capacity, dtype=jnp.int32)
        chosen = wanted[:, :, None] * (order[:, :, None] == slots).astype(jnp.int32)
        send_index = jnp.sum(chosen * (every % tile_dev)[:, :, None], axis=1).reshape(-1)
        place = jnp.where(is_self, local, tile_dev + source * capacity + rank)
        first_list, second_list = jnp.zeros_like(source), place * tile_rows
        stat_base = (tile_dev + peers * capacity) * tile_rows
        slots = [(0, stat_base + d * STAT_ROWS) for d in range(peers)]

        def exchange(piece, contract, near):
            tiles = piece[:rows].reshape(tile_dev, tile_rows, columns)
            incoming = lax.all_to_all(tiles[send_index], "sector", 0, 0, tiled=True)
            stats = lax.all_gather(piece[rows:], "sector", axis=0, tiled=True)
            buffer = jnp.concatenate([piece[:rows], incoming.reshape(-1, columns), stats], axis=0)
            near = prepare(piece) if near is None else near
            return [buffer], near, contract(0, buffer, near, [])

    vmem = pl.BlockSpec(memory_space=pltpu.VMEM)
    smem = pl.BlockSpec(memory_space=pltpu.SMEM)
    hbm = pl.BlockSpec(memory_space=pltpu.HBM)

    piece = pl.pallas_call(
        start_kernel,
        out_shape=jax.ShapeDtypeStruct((piece_rows, columns), bf16),
        in_specs=[vmem],
        out_specs=vmem,
        compiler_params=pltpu.CompilerParams(vmem_limit_bytes=4 * 2**20),
    )(wavefunction)
    phases = max(p for p, _ in slots) + 1
    env_flat = env_left.reshape(tile_dev * terms * tile_rows, tile_rows)
    right_flat = right_environment_terms.reshape(terms * columns, columns)
    left_type = pltpu.VMEM((shifts * rows, (terms // shifts) * columns), bf16)

    def prepare(marker):
        tied = lax.optimization_barrier((own, first_list, second_list, env_flat, marker))
        counts, lists, places, env_near = pl.pallas_call(
            functools.partial(prepare_kernel, sizes, phases, peers, use_ring),
            out_shape=(
                pltpu.SMEM((phases,), jnp.int32),
                pltpu.SMEM((3, phases * records), jnp.int32),
                pltpu.SMEM((peers,), jnp.int32),
                pltpu.VMEM(env_flat.shape, bf16),
            ),
            in_specs=[smem, hbm, hbm, hbm],
            out_specs=(smem, smem, smem, vmem),
            scratch_shapes=[
                pltpu.SMEM((records,), jnp.int32),
                pltpu.SMEM((records,), jnp.int32),
                pltpu.SemaphoreType.DMA((3,)),
            ],
            compiler_params=pltpu.CompilerParams(vmem_limit_bytes=40 * 2**20),
        )(tied[0].reshape(1), *tied[1:4])
        return env_near, right_flat, counts, lists, places

    def contract(phase, buffer, near, held, *more):
        env_near, right_near, counts, lists, places = near
        return pl.pallas_call(
            functools.partial(left_kernel, phase, 10 if phase > peers - 5 else 4, sizes),
            out_shape=left_type,
            in_specs=[smem, smem] + [vmem] * (2 + len(held) + len(more)),
            out_specs=vmem,
            input_output_aliases={4: 0} if held else {},
            compiler_params=pltpu.CompilerParams(vmem_limit_bytes=4 * 2**20),
            cost_estimate=pl.CostEstimate(
                flops=2**32 if phase == 0 and not held else 2**29,
                bytes_accessed=2**20,
                transcendentals=0,
            ),
        )(counts, lists, buffer, env_near, *held, *more)

    def apply_operator(stage, buffers, near, held, prior, coefs):
        image = pltpu.VMEM((rows, columns), f32)
        small = jax.ShapeDtypeStruct((8, 128), f32)
        send = small if stage == 3 else jax.ShapeDtypeStruct((piece_rows, columns), bf16)
        env_near, right_near, counts, lists, places = near
        operands = [right_near, wavefunction, *buffers, *prior, *coefs, held]
        return pl.pallas_call(
            functools.partial(apply_kernel, stage, sizes, slots),
            out_shape=(image, small, send),
            in_specs=[smem] + [vmem] * len(operands),
            out_specs=(vmem, vmem, vmem),
            scratch_shapes=[pltpu.VMEM((peers * STAT_ROWS, 128), bf16)],
            compiler_params=pltpu.CompilerParams(vmem_limit_bytes=12 * 2**20),
            cost_estimate=pl.CostEstimate(
                flops=4 * rows * terms * tile_rows * columns, bytes_accessed=2**24, transcendentals=0
            ),
        )(places, *operands)

    buffers, near, left = exchange(piece, contract, None)
    image_one, coefs_one, piece = apply_operator(1, buffers, near, left, [], [])
    buffers, near, left = exchange(piece, contract, near)
    image_two, coefs_two, piece = apply_operator(2, buffers, near, left, [image_one], [coefs_one])
    buffers, near, left = exchange(piece, contract, near)
    image_three, coefs_three, stats = apply_operator(
        3, buffers, near, left, [image_one, image_two], [coefs_two]
    )
    distance = peers // 2
    while distance:
        pairs = [(i, i ^ distance) for i in range(peers)]
        stats = stats + lax.ppermute(stats, "sector", pairs)
        distance //= 2
    projected = pl.pallas_call(
        functools.partial(finish_kernel, total),
        out_shape=jax.ShapeDtypeStruct((3, 3), f32),
        in_specs=[vmem, vmem],
        out_specs=vmem,
        compiler_params=pltpu.CompilerParams(vmem_limit_bytes=2 * 2**20),
    )(stats, coefs_three)
    return (image_three, projected)


def solution(mesh):
    return jax.shard_map(
        per_device,
        mesh=mesh,
        in_specs=(
            P(("groups", "sector"), None),
            P(("groups", "sector"), None, None, None),
            P("groups", None, None),
            P("groups", None),
        ),
        out_specs=(P(("groups", "sector"), None), P("groups", None)),
        check_vma=False,
    )
```
